512 devices in a mesh: dp: 8 (over y, x_hi), expert: 64 (over z, x_lo, core).
Axes of the slice: x: 4 (x_hi: 2, x_lo: 2; x = x_hi * 2 + x_lo), y: 4, z: 16, core: 2. Of those that a mesh axis runs over, the one named last changes fastest.
Arguments:
- activations: bfloat16 [65536, 2048], P(('dp', 'expert')), may hold values from -6 to 6
- routes: int32 [65536, 8], P(('dp', 'expert')), may hold values from 0 to 63, all different within a row; in each aligned block of 128 rows (0 to 127, 128 to 255, ...) at most 18 rows name the same one
- gate_probs: float32 [65536, 8], P(('dp', 'expert')), may hold values from 0.1 to 1
- advantage: float32 [65536], P(('dp', 'expert')), may hold values from -6 to 6
- readout: bfloat16 [64, 768], replicated, may hold values from -6 to 6
- weights: bfloat16 [64, 2048, 768], P('expert', 'dp'), may hold values from -6 to 6
- moment_one: float32 [64, 2048, 768], P('expert', 'dp'), may hold values from -4 to 4
- moment_two: float32 [64, 2048, 768], P('expert', 'dp'), may hold values from 0.05 to 2
- swap_flags: int32 [64], replicated, may hold values from 0 to 1, as said below
Outputs:
- new_weights: bfloat16 [64, 2048, 768], P('expert', 'dp')
- new_moment_one: float32 [64, 2048, 768], P('expert', 'dp')
- new_moment_two: float32 [64, 2048, 768], P('expert', 'dp')
The draws below stay inside these ranges and needn't reach their ends.
Inputs may be any that keep to these rules, and one draw needn't show every extreme that they name: `routes`: each row names 8 different experts, and the rows of one device name any expert at most 18 times. swap_flags[j] equals swap_flags[(j + 32) mod 64]: partners trade together.
All inputs are finite; a program needn't handle non-finite values.
Results may differ from the reference program's by a relative error of at most 0.0085.
Values may be sent and summed in bfloat16 or wider, within the bound.
No kernel may reach another device: no remote copies, remote signals or barrier semaphores. Data moves between devices by JAX's collectives and lax.ppermute only.
A program may use at most 64 MiB of HBM per device.

```python
import math
import jax
import jax.numpy as jnp
import numpy as np
from jax import lax

D = 2048
FF = 768
TOP = 8
TOK_DEV = 128
EXPERTS = 64
CAP = 18
TOKENS = 65536
N_DP = 8


def draw_swap_flags(key, part):
    key = jax.random.fold_in(key, 7)
    halves = jax.random.randint(key, (EXPERTS // 2,), 0, 2)
    halves = halves.at[0].set(1).at[1].set(0)
    return jnp.concatenate([halves, halves]).astype(jnp.int32)


def block_levels(rng, dims, shards, low, largest):
    def one(position, parts):
        draws = jax.random.uniform(jax.random.fold_in(jax.random.fold_in(rng, 6), position), (parts,), jnp.float32, low / len(shards), largest / len(shards))
        return jnp.repeat(jnp.exp(draws), dims[position] // parts).reshape((-1,) + (1,) * (len(dims) - position - 1))

    gain = one(*shards[0])
    for cut in shards[1:]:
        gain = gain * one(*cut)
    return gain


def shared_out(rng, own, number, rows, number_of, top, bound, skew):
    order = jax.random.permutation(rng, number_of)
    packed, ordinary = portions_of(number_of, rows * top, bound, skew, True), portions_of(number_of, rows * top, bound, skew, False)
    places = jnp.arange(number_of)

    def named(tallies, rotation):
        used = int((tallies > 0).sum())
        fixed = max(1, used // 4)
        moved = fixed + (places - fixed + rotation * (used - fixed)) % max(1, number_of - fixed)
        return jnp.zeros((number_of,), jnp.int32).at[order[jnp.where(places < fixed, places, moved)]].set(jnp.asarray(tallies, jnp.int32))

    tallies = jnp.where(number % 4 == 0, named(packed, number // 4), named(ordinary, number - number // 4 - 1))
    mixed = jax.random.permutation(jax.random.fold_in(own, 3), number_of)
    giver, receiver = mixed[0:number_of // 2 * 2:2], mixed[1:number_of // 2 * 2:2]
    slack = jnp.minimum(tallies[giver] - 1, bound - tallies[receiver]) // 2
    slack = jnp.where((giver == order[0]) | (receiver == order[0]) | (tallies[receiver] == 0), 0, jnp.maximum(slack, 0))
    moved = jax.random.randint(jax.random.fold_in(own, 4), (number_of // 2,), 0, 1 << 20) % (slack + 1)
    tallies = tallies.at[giver].add(-moved).at[receiver].add(moved)
    members = jnp.searchsorted(jnp.cumsum(tallies), jnp.arange(rows * top), side="right").astype(jnp.int32)
    table = members.reshape(top, rows).T
    table = table[jax.random.permutation(jax.random.fold_in(own, 1), rows)]
    rotation = jax.random.randint(jax.random.fold_in(own, 2), (rows, 1), 0, top)
    return jnp.take_along_axis(table, (jnp.arange(top)[None, :] + rotation) % top, axis=1)


def portions_of(number_of, total, bound, lean, full):
    weights = [(1 << 20) // math.isqrt(rank ** lean) + 1 for rank in range(1, number_of + 1)]
    largest = bound if full else min(bound, max(-(-total // number_of), total * weights[0] // sum(weights)))
    least = 1 if total - largest >= number_of - 1 else 0
    holding, rest = [largest] + [least] * (number_of - 1), total - largest - least * (number_of - 1)
    while rest > 0:
        candidates = [i for i in range(1, number_of) if holding[i] < largest] or [i for i in range(1, number_of) if holding[i] < bound]
        whole, remaining = sum([weights[i] for i in candidates]), rest
        for i in candidates:
            extra = min(bound - holding[i], max(1, remaining * weights[i] // whole), rest)
            holding[i] = holding[i] + extra
            rest = rest - extra
    return np.array(holding)


def centred(key, extent, spread, bound, shards=(), kind=jnp.bfloat16):
    result = spread * jax.random.normal(key, extent, jnp.float32)
    if shards:
        result = result * block_levels(key, extent, shards, -0.22, 0.18)
    return jnp.clip(result, -bound, bound).astype(kind)


def setup_inputs(seed: int = 0) -> dict:
    key_list = jax.random.split(jax.random.key(seed), 10)
    activations = centred(key_list[0], (TOKENS, D), 1.0, 6.0, ((0, 512),))
    routes_keys = jax.random.split(jax.random.fold_in(key_list[1], 1), TOKENS // TOK_DEV)
    routes_turns = jax.random.permutation(jax.random.fold_in(key_list[1], 3), TOKENS // TOK_DEV)
    routes = jax.vmap(lambda own, number: shared_out(jax.random.fold_in(key_list[1], 2), own, number, TOK_DEV, EXPERTS, TOP, CAP, 2))(routes_keys, routes_turns).reshape((TOKENS, TOP))
    gate_probs = jnp.clip(0.1 + 0.9 * jax.random.uniform(key_list[2], (TOKENS, TOP), jnp.float32) ** block_levels(key_list[2], (TOKENS, TOP), ((0, 512),), -0.2, 0.2), 0.1, 1.0)
    advantage = centred(key_list[3], (TOKENS,), 1.0, 6.0, ((0, 512),), jnp.float32)
    readout = centred(key_list[4], (EXPERTS, FF), 1.0, 6.0)
    weights = centred(key_list[5], (EXPERTS, D, FF), 1.0, 6.0, ((0, 64), (1, 8)))
    moment_one = centred(key_list[6], (EXPERTS, D, FF), 0.5, 4.0, ((0, 64), (1, 8)), jnp.float32)
    moment_two = jnp.clip(jnp.exp(math.log(2.0) - 3.6888794 * jax.random.uniform(key_list[7], (EXPERTS, D, FF), jnp.float32) ** block_levels(key_list[7], (EXPERTS, D, FF), ((0, 64), (1, 8)), -0.2, 0.2)), 0.05, 2.0)
    swap_flags = draw_swap_flags(jax.random.fold_in(key_list[9], 71), 0)
    return dict(activations=activations, routes=routes, gate_probs=gate_probs, advantage=advantage, readout=readout, weights=weights, moment_one=moment_one, moment_two=moment_two, swap_flags=swap_flags)


beta_one = 0.9
beta_two = 0.95
learn_rate = 0.02
epsilon = 1e-08
decay_rate = 0.1
adam_step = 10.0

def silu_slope(preact):
    sigmoid_val = jax.nn.sigmoid(preact)
    return sigmoid_val * (1.0 + preact * (1.0 - sigmoid_val))

def reference(activations, routes, gate_probs, advantage, readout, weights, moment_one, moment_two, swap_flags):
    inv_root = 1.0 / math.sqrt(D)
    block_rows = EXPERTS * TOK_DEV
    slot_total = EXPERTS * CAP
    factor = (advantage[:, None] * gate_probs).astype(jnp.bfloat16)
    act_blocks = activations.reshape(N_DP, block_rows, D)
    route_blocks = routes.reshape(N_DP, block_rows, TOP)
    factor_blocks = factor.reshape(N_DP, block_rows, TOP)

    def expert_grad(expert):
        weight = weights[expert]
        readout_row = readout[expert].astype(jnp.float32)
        running = jnp.zeros((D, FF), jnp.float32)
        for which_block in range(N_DP):
            matches = route_blocks[which_block] == expert
            chosen = jnp.any(matches, axis=1)
            slot_factor = lax.optimization_barrier(jnp.sum(jnp.where(matches, factor_blocks[which_block].astype(jnp.float32), 0.0), axis=1))
            picked = jnp.nonzero(chosen, size=slot_total, fill_value=0)[0].astype(jnp.int32)
            in_use = jnp.arange(slot_total, dtype=jnp.int32) < jnp.sum(chosen.astype(jnp.int32))
            gathered = jnp.take(act_blocks[which_block], picked, axis=0)
            factors = jnp.where(in_use, jnp.take(slot_factor, picked), 0.0)
            preact = jnp.dot(gathered, weight, preferred_element_type=jnp.float32) * inv_root
            slopes = (factors[:, None] * readout_row[None, :] * silu_slope(preact)).astype(jnp.bfloat16)
            partial_value = jnp.dot(gathered.T, slopes, preferred_element_type=jnp.float32) * inv_root
            rounded = lax.optimization_barrier(partial_value.astype(jnp.bfloat16))
            running = running + rounded.astype(jnp.float32)
        return running
    gradients = lax.map(expert_grad, jnp.arange(EXPERTS, dtype=jnp.int32))
    first = beta_one * moment_one + (1.0 - beta_one) * gradients
    second = beta_two * moment_two + (1.0 - beta_two) * gradients * gradients
    first_hat = first / (1.0 - beta_one ** adam_step)
    second_hat = second / (1.0 - beta_two ** adam_step)
    old_weight = weights.astype(jnp.float32)
    updated = (old_weight - learn_rate * (first_hat / (jnp.sqrt(second_hat) + epsilon) + decay_rate * old_weight)).astype(jnp.bfloat16)
    resident = (jnp.arange(EXPERTS, dtype=jnp.int32) + swap_flags * (EXPERTS // 2)) % EXPERTS
    return (jnp.take(updated, resident, axis=0), jnp.take(first, resident, axis=0), jnp.take(second, resident, axis=0))
```

```python
import math

import jax
import jax.numpy as jnp
from jax import lax
from jax.sharding import Mesh, PartitionSpec as P

beta_one = 0.9
beta_two = 0.95
learn_rate = 0.02
epsilon = 1e-08
decay_rate = 0.1
adam_step = 10.0

NY, NH, NZ, NX, NC = 4, 2, 16, 2, 2
CAP = 18
RELS = ((0, 0), (0, 1), (1, 0), (1, 1))
GROUPS = ((0, 1, -1, 2, -2), (3, -3, 4, -4), (5, -5, 6, -6), (7, -7, 8))


def shift_z(block, distance):
    return lax.ppermute(block, "z", [(i, (i + distance) % NZ) for i in range(NZ)])


def swap_xc(block, dx, dc):
    pairs = [
        (x * NC + c, (x ^ dx) * NC + (c ^ dc)) for x in range(NX) for c in range(NC)
    ]
    return lax.ppermute(block, ("x", "c"), pairs)


def shift_dp(block, dy, dh):
    pairs = [
        (y * NH + h, ((y + dy) % NY) * NH + (h + dh) % NH)
        for y in range(NY)
        for h in range(NH)
    ]
    return lax.ppermute(block, ("y", "h"), pairs)


def silu_slope(preact):
    sigmoid_val = jax.nn.sigmoid(preact)
    return sigmoid_val * (1.0 + preact * (1.0 - sigmoid_val))


def adam_update(weight_now, first_now, second_now, gradient):
    first = beta_one * first_now + (1.0 - beta_one) * gradient
    second = beta_two * second_now + (1.0 - beta_two) * gradient * gradient
    first_hat = first / (1.0 - beta_one**adam_step)
    second_hat = second / (1.0 - beta_two**adam_step)
    old_weight = weight_now.astype(jnp.float32)
    updated = (
        old_weight
        - learn_rate * (first_hat / (jnp.sqrt(second_hat) + epsilon) + decay_rate * old_weight)
    ).astype(jnp.bfloat16)
    return (updated, first, second)


def body(
    activations, routes, gate_probs, advantage, readout, weights, moment_one, moment_two, swap_flags
):
    tok_rows, width_d = activations.shape
    experts = NZ * NX * NC
    half = experts // 2
    inv_root = 1.0 / math.sqrt(width_d)
    z, x, c = lax.axis_index("z"), lax.axis_index("x"), lax.axis_index("c")
    y, h = lax.axis_index("y"), lax.axis_index("h")
    position = (z * NX + x) * NC + c

    def home(index):
        flag = lax.dynamic_index_in_dim(swap_flags, index, 0, keepdims=False)
        return (index + flag * half) % experts, flag

    resident, my_flag = home(position)

    weight_own = weights[0]
    weight_far = shift_z(weight_own, NZ // 2)
    weight_now = jnp.where(my_flag == 1, weight_far, weight_own)
    weight_full = lax.all_gather(weight_now, ("y", "h"), axis=0, tiled=True)

    blocks = {0: activations}
    fwd = bwd = activations
    for k in range(1, NZ // 2):
        fwd = shift_z(fwd, 1)
        bwd = shift_z(bwd, -1)
        blocks[-k] = fwd
        blocks[k] = bwd
    half_rows = tok_rows // 2
    blocks[8] = jnp.concatenate(
        [shift_z(fwd[:half_rows], 1), shift_z(bwd[half_rows:], -1)], axis=0
    )

    factor = (advantage[:, None] * gate_probs).astype(jnp.bfloat16)
    meta = jnp.concatenate([routes.astype(jnp.bfloat16).T, factor.T], axis=0)
    meta_all = lax.all_gather(meta, ("z", "x", "c"), axis=0, tiled=False)
    meta_all = meta_all.reshape(NZ, NX, NC, 2, 8, tok_rows)
    meta_all = jnp.concatenate([meta_all, meta_all], axis=0)
    offsets = [o % NZ for group in GROUPS for o in group]
    meta_z = lax.dynamic_slice_in_dim(meta_all, z, NZ, 0)
    meta_z = jnp.stack([meta_z[o] for o in offsets])
    by_rel = []
    for dx, dc in RELS:
        part = lax.dynamic_index_in_dim(meta_z, x ^ dx, 1, keepdims=False)
        by_rel.append(lax.dynamic_index_in_dim(part, c ^ dc, 1, keepdims=False))
    routes_rel = jnp.stack([m[:, 0] for m in by_rel], axis=1)
    factor_rel = jnp.stack([m[:, 1] for m in by_rel], axis=1).astype(jnp.float32)
    dest_home = jnp.stack(
        [home((z * NX + (x ^ dx)) * NC + (c ^ dc))[0] for dx, dc in RELS]
    ).astype(jnp.bfloat16)
    tri = (
        jnp.arange(tok_rows)[:, None] < jnp.arange(tok_rows)[None, :]
    ).astype(jnp.bfloat16)

    def ranked(mask):
        rank = lax.dot_general(
            mask.astype(jnp.bfloat16),
            tri,
            (((2,), (0,)), ((), ())),
            preferred_element_type=jnp.float32,
        )
        return jnp.where(mask, rank.astype(jnp.int32), -1000)

    out_mask = jnp.any(
        routes_rel[:, 0, None] == dest_home[None, :, None, None], axis=2
    )
    out_rank = ranked(out_mask)
    in_hot = routes_rel == resident.astype(jnp.bfloat16)
    in_rank = ranked(jnp.any(in_hot, axis=2))
    in_factor = jnp.sum(jnp.where(in_hot, factor_rel, 0.0), axis=2)

    readout_row = lax.dynamic_index_in_dim(readout, resident, 0, keepdims=False).astype(jnp.float32)

    all_rows, all_slopes = [], []
    start = 0
    for group in GROUPS:
        count = len(group)
        rows = -(-count * CAP // 8) * 8
        base = (jnp.arange(count, dtype=jnp.int32) * CAP)[:, None, None]
        slots = jnp.arange(rows, dtype=jnp.int32)
        mine = out_rank[start : start + count] + base
        select = (
            mine.transpose(1, 0, 2)[:, None] == slots[None, :, None, None]
        ).astype(jnp.bfloat16)
        theirs = in_rank[start : start + count] + base
        slot_factor = jnp.sum(
            jnp.where(
                theirs.transpose(1, 0, 2)[:, None] == slots[None, :, None, None],
                in_factor[start : start + count].transpose(1, 0, 2)[:, None],
                0.0,
            ),
            axis=(2, 3),
        ).reshape(4 * rows, 1)
        source = jnp.concatenate([blocks[o] for o in group], axis=0)
        picked = jnp.dot(
            select.reshape(4 * rows, count * tok_rows),
            source,
            preferred_element_type=jnp.float32,
        ).astype(jnp.bfloat16)
        pieces = [
            picked[i * rows : (i + 1) * rows]
            if rel == (0, 0)
            else swap_xc(picked[i * rows : (i + 1) * rows], *rel)
            for i, rel in enumerate(RELS)
        ]
        slot_rows = jnp.concatenate(pieces, axis=0)
        preact = (
            jnp.dot(slot_rows, weight_full, preferred_element_type=jnp.float32) * inv_root
        )
        slopes = (slot_factor * readout_row[None, :] * silu_slope(preact)).astype(jnp.bfloat16)
        all_rows.append(slot_rows)
        all_slopes.append(slopes)
        start += count

    moments = jnp.stack([moment_one[0], moment_two[0]]).astype(jnp.bfloat16)
    moments, _ = lax.optimization_barrier((moments, blocks[8]))
    moments_far = shift_z(moments, NZ // 2)

    full_grad = (
        lax.dot_general(
            jnp.concatenate(all_rows, axis=0),
            jnp.concatenate(all_slopes, axis=0),
            (((0,), (0,)), ((), ())),
            preferred_element_type=jnp.float32,
        )
        * inv_root
    ).astype(jnp.bfloat16)
    shard = weight_own.shape[0]

    def part(dy, dh):
        index = ((y + dy) % NY) * NH + (h + dh) % NH
        return lax.dynamic_slice_in_dim(full_grad, index * shard, shard, 0)

    gradient = part(0, 0).astype(jnp.float32)
    for dy, dh in ((2, 1), (1, 1), (3, 1), (2, 0), (1, 0), (3, 0), (0, 1)):
        gradient = gradient + shift_dp(part(dy, dh), dy, dh).astype(jnp.float32)

    first_now = jnp.where(my_flag == 1, moments_far[0].astype(jnp.float32), moment_one[0])
    second_now = jnp.where(my_flag == 1, moments_far[1].astype(jnp.float32), moment_two[0])
    updated, first, second = adam_update(weight_now, first_now, second_now, gradient)
    return (updated[None], first[None], second[None])


def solution(mesh):
    inner = Mesh(mesh.devices.reshape(NY, NH, NZ, NX, NC), ("y", "h", "z", "x", "c"))
    dp, expert = ("y", "h"), ("z", "x", "c")
    placed = (
        P(dp + expert, None),
        P(dp + expert, None),
        P(dp + expert, None),
        P(dp + expert),
        P(),
        P(expert, dp, None),
        P(expert, dp, None),
        P(expert, dp, None),
        P(),
    )
    return jax.shard_map(
        body,
        mesh=inner,
        in_specs=placed,
        out_specs=(P(expert, dp, None),) * 3,
        check_vma=False,
    )
```

```python
import functools
import math

import jax
import jax.numpy as jnp
from jax import lax
from jax.experimental import pallas as pl
from jax.experimental.pallas import tpu as pltpu
from jax.sharding import Mesh, PartitionSpec as P

beta_one = 0.9
beta_two = 0.95
learn_rate = 0.02
epsilon = 1e-08
decay_rate = 0.1
adam_step = 10.0

NY, NH, NZ, NX, NC = 4, 2, 16, 2, 2
CAP = 18
TOK, D, FF = 128, 2048, 768
SHARD = D // (NY * NH)
META = 8
WIDE = D + 128
RELS = ((0, 0), (0, 1), (1, 0), (1, 1))
GROUPS = ((0, 1, -1, 2, -2, 3, -3), (4, -4, 5, -5, 6, -6), (7, -7, 8))
INV_ROOT = 1.0 / math.sqrt(D)
SENDS = ((2, 1), (1, 1), (3, 1), (2, 0), (1, 0), (3, 0), (0, 1), (0, 0))
VMEM_LIMIT = 50 * 1024 * 1024


def rows_of(count):
    return -(-count * CAP // 16) * 16


def shift_z(block, distance):
    return lax.ppermute(block, "z", [(i, (i + distance) % NZ) for i in range(NZ)])


def swap_xc(block, dx, dc):
    pairs = [
        (x * NC + c, (x ^ dx) * NC + (c ^ dc)) for x in range(NX) for c in range(NC)
    ]
    return lax.ppermute(block, ("x", "c"), pairs)


def shift_dp(block, dy, dh):
    pairs = [
        (y * NH + h, ((y + dy) % NY) * NH + (h + dh) % NH)
        for y in range(NY)
        for h in range(NH)
    ]
    return lax.ppermute(block, ("y", "h"), pairs)


def silu_slope(preact):
    sigmoid_val = jax.nn.sigmoid(preact)
    return sigmoid_val * (1.0 + preact * (1.0 - sigmoid_val))


def adam_update(weight_now, first_now, second_now, gradient):
    first = beta_one * first_now + (1.0 - beta_one) * gradient
    second = beta_two * second_now + (1.0 - beta_two) * gradient * gradient
    first_hat = first / (1.0 - beta_one**adam_step)
    second_hat = second / (1.0 - beta_two**adam_step)
    old_weight = weight_now.astype(jnp.float32)
    updated = (
        old_weight
        - learn_rate * (first_hat / (jnp.sqrt(second_hat) + epsilon) + decay_rate * old_weight)
    ).astype(jnp.bfloat16)
    return (updated, first, second)


def select_kernel(cuts, rows, home_ref, *refs):
    outs = refs[-4:]
    count = len(cuts)
    parts, routes, factors, at = [], [], [], 0
    for cut in cuts:
        mine = refs[at : at + cut]
        at += cut
        parts += [(r, min(r.shape[0], TOK if cut == 1 else TOK // cut)) for r in mine]
        tail = mine[-1]
        facts = tail[tail.shape[0] - META :, 0 : 2 * TOK].astype(jnp.float32)
        routes.append(facts[:, :TOK])
        factors.append(facts[:, TOK:])
    masks, gains = [], []
    for i in range(4):
        home = home_ref[i].astype(jnp.float32)
        for b in range(count):
            hot = routes[b] == home
            masks.append(jnp.max(jnp.where(hot, 1.0, 0.0), axis=0, keepdims=True))
            gains.append(jnp.sum(jnp.where(hot, factors[b], 0.0), axis=0, keepdims=True))
    mask = jnp.concatenate(masks, axis=0)
    earlier = (
        lax.broadcasted_iota(jnp.int32, (TOK, TOK), 0)
        < lax.broadcasted_iota(jnp.int32, (TOK, TOK), 1)
    )
    rank = jnp.dot(
        mask.astype(jnp.bfloat16),
        jnp.where(earlier, 1.0, 0.0).astype(jnp.bfloat16),
        preferred_element_type=jnp.float32,
    )
    slots = lax.broadcasted_iota(jnp.int32, (rows, TOK), 0).astype(jnp.float32)
    selects = []
    for i in range(4):
        lanes, total = [], jnp.zeros((rows, 1), jnp.float32)
        for b in range(count):
            at = i * count + b
            slot = jnp.where(mask[at : at + 1] > 0.0, rank[at : at + 1] + float(b * CAP), -1.0)
            one = jnp.where(slots == slot, 1.0, 0.0)
            total = total + jnp.sum(one * gains[at], axis=1, keepdims=True)
            lanes.append(one.astype(jnp.bfloat16))
        selects.append(jnp.concatenate(lanes, axis=1))
        outs[i][:, D:] = jnp.broadcast_to(total, (rows, WIDE - D)).astype(jnp.bfloat16)
    select = jnp.concatenate(selects, axis=0)
    step = 512
    for j in range(0, D, step):
        source = jnp.concatenate([r[0:n, j : j + step] for r, n in parts], axis=0)
        picked = jnp.dot(select, source, preferred_element_type=jnp.float32).astype(jnp.bfloat16)
        for i in range(4):
            outs[i][:, j : j + step] = picked[i * rows : (i + 1) * rows]


def select(blocks, homes):
    cuts = tuple(len(b) for b in blocks)
    rows = rows_of(len(blocks))
    flat = [a for b in blocks for a in b]
    return pl.pallas_call(
        functools.partial(select_kernel, cuts, rows),
        out_shape=[jax.ShapeDtypeStruct((rows, WIDE), jnp.bfloat16)] * 4,
        in_specs=[pl.BlockSpec(memory_space=pltpu.SMEM)]
        + [pl.BlockSpec(memory_space=pltpu.VMEM)] * len(flat),
        out_specs=[pl.BlockSpec(memory_space=pltpu.VMEM)] * 4,
        compiler_params=pltpu.CompilerParams(vmem_limit_bytes=VMEM_LIMIT),
        cost_estimate=pl.CostEstimate(
            flops=2 * 4 * rows * len(blocks) * TOK * D,
            bytes_accessed=2 * D * (len(blocks) * TOK + 4 * rows),
            transcendentals=0,
        ),
        name="select",
    )(homes, *flat)


def slopes_kernel(*refs):
    pieces, weight_ref, readout_ref, out_ref = refs[:4], refs[4], refs[5], refs[6]
    rows = jnp.concatenate([p[:, :D] for p in pieces], axis=0)
    factor = jnp.concatenate([p[:, D : D + 1] for p in pieces], axis=0).astype(jnp.float32)
    step = 256
    for j in range(0, FF, step):
        preact = (
            jnp.dot(rows, weight_ref[:, j : j + step], preferred_element_type=jnp.float32)
            * INV_ROOT
        )
        out_ref[:, j : j + step] = (
            factor * readout_ref[:, j : j + step] * silu_slope(preact)
        ).astype(jnp.bfloat16)


def slopes_of(pieces, weight_full, readout_row):
    rows = 4 * pieces[0].shape[0]
    return pl.pallas_call(
        slopes_kernel,
        out_shape=jax.ShapeDtypeStruct((rows, FF), jnp.bfloat16),
        in_specs=[pl.BlockSpec(memory_space=pltpu.VMEM)] * 6,
        out_specs=pl.BlockSpec(memory_space=pltpu.VMEM),
        compiler_params=pltpu.CompilerParams(vmem_limit_bytes=VMEM_LIMIT),
        cost_estimate=pl.CostEstimate(
            flops=2 * rows * D * FF,
            bytes_accessed=2 * (D * FF + rows * (D + FF)),
            transcendentals=rows * FF,
        ),
        name="slopes",
    )(*pieces, weight_full, readout_row)


def gradient_kernel(n_pieces, order_ref, *refs):
    pieces, slopes, out_ref = refs[:n_pieces], refs[n_pieces:-1], refs[-1]
    rows = jnp.concatenate([p[...] for p in pieces], axis=0)
    down = jnp.concatenate([s[...] for s in slopes], axis=0)
    total = lax.dot_general(
        rows, down, (((0,), (0,)), ((), ())), preferred_element_type=jnp.float32
    )
    out_ref[0] = (total * INV_ROOT).astype(jnp.bfloat16)


def gradient_parts(pieces, slopes, order):
    parts = order.shape[0]
    rows = sum(p.shape[0] for p in pieces)
    return pl.pallas_call(
        functools.partial(gradient_kernel, len(pieces)),
        out_shape=jax.ShapeDtypeStruct((parts, SHARD, FF), jnp.bfloat16),
        grid_spec=pltpu.PrefetchScalarGridSpec(
            num_scalar_prefetch=1,
            grid=(parts,),
            in_specs=[
                pl.BlockSpec((p.shape[0], SHARD), lambda i, order: (0, order[i])) for p in pieces
            ]
            + [pl.BlockSpec(s.shape, lambda i, order: (0, 0)) for s in slopes],
            out_specs=pl.BlockSpec((1, SHARD, FF), lambda i, order: (i, 0, 0)),
        ),
        compiler_params=pltpu.CompilerParams(
            vmem_limit_bytes=VMEM_LIMIT, dimension_semantics=("arbitrary",)
        ),
        cost_estimate=pl.CostEstimate(
            flops=2 * rows * parts * SHARD * FF,
            bytes_accessed=2 * (rows * (parts * SHARD + FF) + parts * SHARD * FF),
            transcendentals=0,
        ),
        name="gradient",
    )(order, *pieces, *slopes)


def body(
    activations, routes, gate_probs, advantage, readout, weights, moment_one, moment_two, swap_flags
):
    experts = NZ * NX * NC
    half = experts // 2
    z, x, c = lax.axis_index("z"), lax.axis_index("x"), lax.axis_index("c")
    y, h = lax.axis_index("y"), lax.axis_index("h")

    def home(dx, dc):
        index = (z * NX + (x ^ dx)) * NC + (c ^ dc)
        flag = lax.dynamic_index_in_dim(swap_flags, index, 0, keepdims=False)
        return (index + flag * half) % experts, flag

    resident, my_flag = home(0, 0)
    homes = jnp.stack([home(dx, dc)[0] for dx, dc in RELS])

    weight_own = weights[0]
    weight_far = shift_z(weight_own, NZ // 2)
    weight_now = jnp.where(my_flag == 1, weight_far, weight_own)
    weight_full = lax.all_gather(weight_now, ("y", "h"), axis=0, tiled=True)

    factor = (advantage[:, None] * gate_probs).astype(jnp.bfloat16)
    facts = jnp.concatenate([routes.astype(jnp.bfloat16).T, factor.T], axis=1)
    facts = jnp.pad(facts, ((0, 0), (0, D - 2 * TOK)))
    block = jnp.concatenate([activations, facts], axis=0)
    blocks = {0: (block,)}
    fwd = bwd = block
    for k in range(1, NZ // 2):
        fwd = shift_z(fwd, 1)
        bwd = shift_z(bwd, -1)
        blocks[-k] = (fwd,)
        blocks[k] = (bwd,)
    last = (shift_z(fwd[: TOK // 2], 1), shift_z(bwd[TOK // 2 :], -1))
    moments = jnp.stack([moment_one[0], moment_two[0]]).astype(jnp.bfloat16)

    readout_row = lax.dynamic_index_in_dim(readout, resident, 0).astype(jnp.float32)

    all_pieces, all_slopes = [], []
    for number, group in enumerate(GROUPS):
        if number == len(GROUPS) - 1:
            last, moments, all_slopes = lax.optimization_barrier((last, moments, all_slopes))
            blocks[8] = last
        picked = select([blocks[o] for o in group], homes)
        pieces = [
            piece if rel == (0, 0) else swap_xc(piece, *rel) for piece, rel in zip(picked, RELS)
        ]
        all_slopes.append(slopes_of(pieces, weight_full, readout_row))
        all_pieces += pieces

    moments_far = shift_z(moments, NZ // 2)

    order = jnp.stack([((y + dy) % NY) * NH + (h + dh) % NH for dy, dh in SENDS])
    parts = gradient_parts(all_pieces, all_slopes, order)
    gradient = parts[len(SENDS) - 1].astype(jnp.float32)
    for i, (dy, dh) in enumerate(SENDS[:-1]):
        gradient = gradient + shift_dp(parts[i], dy, dh).astype(jnp.float32)

    first_now = jnp.where(my_flag == 1, moments_far[0].astype(jnp.float32), moment_one[0])
    second_now = jnp.where(my_flag == 1, moments_far[1].astype(jnp.float32), moment_two[0])
    updated, first, second = adam_update(weight_now, first_now, second_now, gradient)
    return (updated[None], first[None], second[None])


def solution(mesh):
    inner = Mesh(mesh.devices.reshape(NY, NH, NZ, NX, NC), ("y", "h", "z", "x", "c"))
    dp, expert = ("y", "h"), ("z", "x", "c")
    placed = (
        P(dp + expert, None),
        P(dp + expert, None),
        P(dp + expert, None),
        P(dp + expert),
        P(),
        P(expert, dp, None),
        P(expert, dp, None),
        P(expert, dp, None),
        P(),
    )
    return jax.shard_map(
        body,
        mesh=inner,
        in_specs=placed,
        out_specs=(P(expert, dp, None),) * 3,
        check_vma=False,
    )
```

```python
import functools
import math

import jax
import jax.numpy as jnp
from jax import lax
from jax.experimental import pallas as pl
from jax.experimental.pallas import tpu as pltpu
from jax.sharding import Mesh, PartitionSpec as P

beta_one = 0.9
beta_two = 0.95
learn_rate = 0.02
epsilon = 1e-08
decay_rate = 0.1
adam_step = 10.0

NY, NH, NZ, NX, NC = 4, 2, 16, 2, 2
CAP = 18
TOK, D, FF = 128, 2048, 768
SHARD = D // (NY * NH)
META = 8
WIDE = D + 128
RELS = ((0, 0), (0, 1), (1, 0), (1, 1))
GROUPS = (((0, 1, -1, 2, -2, 3), (-3, 4, -4, 5, -5)), ((6, -6, 7, -7, 8),))
TILE = 512
INV_ROOT = 1.0 / math.sqrt(D)
SENDS = ((2, 1), (1, 1), (3, 1), (2, 0), (1, 0), (3, 0), (0, 1))
CUTS = (SHARD // 8, 7 * SHARD // 8)
VMEM_LIMIT = 56 * 1024 * 1024


def rows_of(count):
    return -(-count * CAP // 16) * 16


def shift_z(block, distance):
    return lax.ppermute(block, "z", [(i, (i + distance) % NZ) for i in range(NZ)])


def swap_xc(block, dx, dc):
    pairs = [
        (x * NC + c, (x ^ dx) * NC + (c ^ dc)) for x in range(NX) for c in range(NC)
    ]
    return lax.ppermute(block, ("x", "c"), pairs)


def shift_dp(block, dy, dh):
    pairs = [
        (y * NH + h, ((y + dy) % NY) * NH + (h + dh) % NH)
        for y in range(NY)
        for h in range(NH)
    ]
    return lax.ppermute(block, ("y", "h"), pairs)


def silu_slope(preact):
    sigmoid_val = jax.nn.sigmoid(preact)
    return sigmoid_val * (1.0 + preact * (1.0 - sigmoid_val))


def cast_kernel(one_ref, two_ref, *outs):
    at = 0
    for out in outs:
        rows = out.shape[1]
        out[0] = one_ref[at : at + rows, :].astype(jnp.bfloat16)
        out[1] = two_ref[at : at + rows, :].astype(jnp.bfloat16)
        at += rows


def cast_moments(one, two):
    step = FF // 2
    return pl.pallas_call(
        cast_kernel,
        out_shape=[jax.ShapeDtypeStruct((2, rows, FF), jnp.bfloat16) for rows in CUTS],
        grid=(FF // step,),
        in_specs=[pl.BlockSpec((SHARD, step), lambda i: (0, i))] * 2,
        out_specs=[pl.BlockSpec((2, rows, step), lambda i: (0, 0, i)) for rows in CUTS],
        compiler_params=pltpu.CompilerParams(vmem_limit_bytes=VMEM_LIMIT),
        cost_estimate=pl.CostEstimate(
            flops=2 * SHARD * FF, bytes_accessed=12 * SHARD * FF, transcendentals=0
        ),
        name="cast",
    )(one, two)


def adam_kernel(n_parts, flag_ref, *refs):
    parts = refs[:n_parts]
    own_ref, weight_ref, one_ref, two_ref = refs[n_parts : n_parts + 4]
    far_a, far_b = refs[n_parts + 4 : n_parts + 6]
    updated_ref, first_ref, second_ref = refs[n_parts + 6 :]
    total = own_ref[0].astype(jnp.float32)
    for part in parts:
        total = total + part[...].astype(jnp.float32)
    gradient = total.T
    swapped = flag_ref[0] == 1
    rows = gradient.shape[0]
    rest = rows - far_a.shape[1]
    low = jnp.concatenate([far_a[...], far_b[:, :rest]], axis=1).astype(jnp.float32)
    high = far_b[:, rest:].astype(jnp.float32)
    far = jnp.where(pl.program_id(0) == 0, low, high)
    first_now = jnp.where(swapped, far[0], one_ref[...])
    second_now = jnp.where(swapped, far[1], two_ref[...])
    first = beta_one * first_now + (1.0 - beta_one) * gradient
    second = beta_two * second_now + (1.0 - beta_two) * gradient * gradient
    first_hat = first / (1.0 - beta_one**adam_step)
    second_hat = second / (1.0 - beta_two**adam_step)
    old_weight = weight_ref[...].astype(jnp.float32)
    updated_ref[...] = (
        old_weight
        - learn_rate * (first_hat / (jnp.sqrt(second_hat) + epsilon) + decay_rate * old_weight)
    ).astype(jnp.bfloat16)
    first_ref[...] = first
    second_ref[...] = second


def adam(flag, own, received, weight, one, two, far):
    step = SHARD // 2
    plain = pl.BlockSpec((step, FF), lambda i: (i, 0))
    whole = [pl.BlockSpec(f.shape, lambda i: (0, 0, 0)) for f in far]
    return pl.pallas_call(
        functools.partial(adam_kernel, len(received)),
        out_shape=[
            jax.ShapeDtypeStruct((SHARD, FF), jnp.bfloat16),
            jax.ShapeDtypeStruct((SHARD, FF), jnp.float32),
            jax.ShapeDtypeStruct((SHARD, FF), jnp.float32),
        ],
        grid=(SHARD // step,),
        in_specs=[pl.BlockSpec(memory_space=pltpu.SMEM)]
        + [pl.BlockSpec((FF, step), lambda i: (0, i))] * len(received)
        + [pl.BlockSpec((1, FF, step), lambda i: (0, 0, i))]
        + [plain, plain, plain]
        + whole,
        out_specs=[plain] * 3,
        compiler_params=pltpu.CompilerParams(vmem_limit_bytes=VMEM_LIMIT),
        cost_estimate=pl.CostEstimate(
            flops=30 * SHARD * FF, bytes_accessed=40 * SHARD * FF, transcendentals=SHARD * FF
        ),
        name="adam",
    )(flag, *received, own, weight, one, two, *far)


def pick_plan(homes, facts, rows):
    count = len(facts)
    masks, gains = [], []
    for home in homes:
        for routes, factors in facts:
            hot = routes == home
            masks.append(jnp.max(jnp.where(hot, 1.0, 0.0), axis=0, keepdims=True))
            gains.append(jnp.sum(jnp.where(hot, factors, 0.0), axis=0, keepdims=True))
    mask = jnp.concatenate(masks, axis=0)
    earlier = (
        lax.broadcasted_iota(jnp.int32, (TOK, TOK), 0)
        < lax.broadcasted_iota(jnp.int32, (TOK, TOK), 1)
    )
    rank = jnp.dot(
        mask.astype(jnp.bfloat16),
        jnp.where(earlier, 1.0, 0.0).astype(jnp.bfloat16),
        preferred_element_type=jnp.float32,
    )
    slots = lax.broadcasted_iota(jnp.int32, (rows, TOK), 0).astype(jnp.float32)
    selects, totals = [], []
    for i in range(len(homes)):
        lanes, total = [], jnp.zeros((rows, 1), jnp.float32)
        for b in range(count):
            at = i * count + b
            slot = jnp.where(mask[at : at + 1] > 0.0, rank[at : at + 1] + float(b * CAP), -1.0)
            one = jnp.where(slots == slot, 1.0, 0.0)
            total = total + jnp.sum(one * gains[at], axis=1, keepdims=True)
            lanes.append(one.astype(jnp.bfloat16))
        selects.append(jnp.concatenate(lanes, axis=1))
        totals.append(total)
    return jnp.concatenate(selects, axis=0), totals


def select_kernel(cuts, home_ref, *refs):
    n_in = sum(sum(cut) for cut in cuts)
    ins, outs, plans = refs[:n_in], refs[n_in : n_in + 4], refs[n_in + 4 : -1]
    gain_ref = refs[-1]
    step = pl.program_id(0)

    @pl.when(step == 0)
    def _():
        homes = [home_ref[i].astype(jnp.float32) for i in range(4)]
        at = row = 0
        for cut, plan in zip(cuts, plans):
            facts = []
            for n in cut:
                tail = ins[at + n - 1]
                found = tail[tail.shape[0] - META :, 0 : 2 * TOK].astype(jnp.float32)
                facts.append((found[:, :TOK], found[:, TOK:]))
                at += n
            rows = rows_of(len(cut))
            chosen, totals = pick_plan(homes, facts, rows)
            plan[...] = chosen
            for i in range(4):
                gain_ref[i, row : row + rows, :] = jnp.broadcast_to(
                    totals[i], (rows, WIDE - D)
                ).astype(jnp.bfloat16)
            row += rows

    @pl.when(step < D // TILE)
    def _():
        at = row = 0
        for cut, plan in zip(cuts, plans):
            parts = []
            for n in cut:
                parts += [r[0 : TOK // n, :] for r in ins[at : at + n]]
                at += n
            rows = rows_of(len(cut))
            picked = jnp.dot(
                plan[...], jnp.concatenate(parts, axis=0), preferred_element_type=jnp.float32
            ).astype(jnp.bfloat16)
            for i in range(4):
                outs[i][row : row + rows, :] = picked[i * rows : (i + 1) * rows]
            row += rows

    @pl.when(step == D // TILE)
    def _():
        for i in range(4):
            outs[i][:, 0 : WIDE - D] = gain_ref[i]


def select(products, homes):
    cuts = tuple(tuple(len(b) for b in blocks) for blocks in products)
    sizes = [rows_of(len(blocks)) for blocks in products]
    rows = sum(sizes)
    flat = [a for blocks in products for b in blocks for a in b]
    last = D // TILE - 1
    return pl.pallas_call(
        functools.partial(select_kernel, cuts),
        out_shape=[jax.ShapeDtypeStruct((rows, WIDE), jnp.bfloat16)] * 4,
        grid=(D // TILE + 1,),
        in_specs=[pl.BlockSpec(memory_space=pltpu.SMEM)]
        + [
            pl.BlockSpec((a.shape[0], TILE), lambda j: (0, jnp.minimum(j, last))) for a in flat
        ],
        out_specs=[pl.BlockSpec((rows, TILE), lambda j: (0, j))] * 4,
        scratch_shapes=[
            pltpu.VMEM((4 * size, len(blocks) * TOK), jnp.bfloat16)
            for size, blocks in zip(sizes, products)
        ]
        + [pltpu.VMEM((4, rows, WIDE - D), jnp.bfloat16)],
        compiler_params=pltpu.CompilerParams(
            vmem_limit_bytes=VMEM_LIMIT, dimension_semantics=("arbitrary",)
        ),
        cost_estimate=pl.CostEstimate(
            flops=sum(8 * s * len(b) * TOK * D for s, b in zip(sizes, products)),
            bytes_accessed=2 * D * (sum(a.shape[0] for a in flat) + 4 * rows),
            transcendentals=0,
        ),
        name="select",
    )(homes, *flat)


def slopes_kernel(*refs):
    pieces, weight_ref, readout_ref, out_ref = refs[:4], refs[4], refs[5], refs[6]
    rows = jnp.concatenate([p[:, :D] for p in pieces], axis=0)
    factor = jnp.concatenate([p[:, D : D + 1] for p in pieces], axis=0).astype(jnp.float32)
    preact = jnp.dot(rows, weight_ref[...], preferred_element_type=jnp.float32) * INV_ROOT
    slope = factor * readout_ref[...] * silu_slope(preact)
    out_ref[...] = slope.T.astype(jnp.bfloat16)


def slopes_of(pieces, weight_full, readout_row):
    rows = 4 * pieces[0].shape[0]
    step = 256
    return pl.pallas_call(
        slopes_kernel,
        out_shape=jax.ShapeDtypeStruct((FF, rows), jnp.bfloat16),
        grid=(FF // step,),
        in_specs=[pl.BlockSpec(p.shape, lambda j: (0, 0)) for p in pieces]
        + [pl.BlockSpec((D, step), lambda j: (0, j)), pl.BlockSpec((1, step), lambda j: (0, j))],
        out_specs=pl.BlockSpec((step, rows), lambda j: (j, 0)),
        compiler_params=pltpu.CompilerParams(vmem_limit_bytes=VMEM_LIMIT),
        cost_estimate=pl.CostEstimate(
            flops=2 * rows * D * FF,
            bytes_accessed=2 * (D * FF + rows * (D + FF)),
            transcendentals=rows * FF,
        ),
        name="slopes",
    )(*pieces, weight_full, readout_row)


def gradient_kernel(n_pieces, *refs):
    pieces, slopes, out_ref = refs[:n_pieces], refs[n_pieces:-1], refs[-1]
    down = jnp.concatenate([s[...] for s in slopes], axis=1)
    rows = jnp.concatenate([p[...] for p in pieces], axis=0)
    total = jnp.dot(down, rows, preferred_element_type=jnp.float32)
    total = (total * INV_ROOT).astype(jnp.bfloat16)
    for i in range(TILE // SHARD):
        out_ref[i] = total[:, i * SHARD : (i + 1) * SHARD]


def gradient_parts(pieces, slopes):
    rows = sum(p.shape[0] for p in pieces)
    return pl.pallas_call(
        functools.partial(gradient_kernel, len(pieces)),
        out_shape=jax.ShapeDtypeStruct((D // SHARD, FF, SHARD), jnp.bfloat16),
        grid=(D // TILE,),
        in_specs=[pl.BlockSpec((p.shape[0], TILE), lambda j: (0, j)) for p in pieces]
        + [pl.BlockSpec(s.shape, lambda j: (0, 0)) for s in slopes],
        out_specs=pl.BlockSpec((TILE // SHARD, FF, SHARD), lambda j: (j, 0, 0)),
        compiler_params=pltpu.CompilerParams(vmem_limit_bytes=VMEM_LIMIT),
        cost_estimate=pl.CostEstimate(
            flops=2 * rows * D * FF,
            bytes_accessed=2 * (rows * (D + FF) + D * FF),
            transcendentals=0,
        ),
        name="gradient",
    )(*pieces, *slopes)


def body(
    activations, routes, gate_probs, advantage, readout, weights, moment_one, moment_two, swap_flags
):
    experts = NZ * NX * NC
    half = experts // 2
    z, x, c = lax.axis_index("z"), lax.axis_index("x"), lax.axis_index("c")
    y, h = lax.axis_index("y"), lax.axis_index("h")

    def home(dx, dc):
        index = (z * NX + (x ^ dx)) * NC + (c ^ dc)
        flag = lax.dynamic_index_in_dim(swap_flags, index, 0, keepdims=False)
        return (index + flag * half) % experts, flag

    resident, my_flag = home(0, 0)
    homes = jnp.stack([home(dx, dc)[0] for dx, dc in RELS])

    factor = (advantage[:, None] * gate_probs).astype(jnp.bfloat16)
    facts = jnp.concatenate([routes.astype(jnp.bfloat16).T, factor.T], axis=1)
    facts = jnp.pad(facts, ((0, 0), (0, D - 2 * TOK)))
    block = jnp.concatenate([activations, facts], axis=0)
    weight_own = weights[0]
    weight_far = shift_z(weight_own, NZ // 2)
    moments = cast_moments(moment_one[0], moment_two[0])
    readout_row = lax.dynamic_index_in_dim(readout, resident, 0).astype(jnp.float32)

    blocks = {0: (block,)}
    fwd = bwd = block
    picked, pieces, slopes, far = [], [], [], []

    def pick(group):
        picked.append(select([[blocks[o] for o in part] for part in group], homes))

    def exchange():
        pieces.append(
            [p if rel == (0, 0) else swap_xc(p, *rel) for p, rel in zip(picked[-1], RELS)]
        )

    for k in range(1, NZ // 2):
        fwd = shift_z(fwd, 1)
        bwd = shift_z(bwd, -1)
        beside = {1: (moments, weight_far), 6: picked[-1:]}.get(k, ())
        fwd, bwd, beside = lax.optimization_barrier((fwd, bwd, beside))
        blocks[-k] = (fwd,)
        blocks[k] = (bwd,)
        if k == 1:
            moments, weight_far = beside
            weight_now = jnp.where(my_flag == 1, weight_far, weight_own)
            weight_full = lax.all_gather(weight_now, ("y", "h"), axis=0, tiled=True)
        elif k == 5:
            pick(GROUPS[0])
        elif k == 6:
            picked[-1] = beside[0]
            exchange()
    last = (shift_z(fwd[: TOK // 2], 1), shift_z(bwd[TOK // 2 :], -1))
    last, moments = lax.optimization_barrier((last, moments))
    blocks[8] = last
    far = [shift_z(m, NZ // 2) for m in moments]
    pick(GROUPS[1])
    exchange()
    slopes = [slopes_of(p, weight_full, readout_row) for p in pieces]
    slopes, far[0] = lax.optimization_barrier((slopes, far[0]))

    parts = gradient_parts([p for group in pieces for p in group], slopes)

    def part(dy, dh):
        index = ((y + dy) % NY) * NH + (h + dh) % NH
        return lax.dynamic_index_in_dim(parts, index, 0)

    received = [shift_dp(part(dy, dh)[0], dy, dh) for dy, dh in SENDS]
    updated, first, second = adam(
        my_flag.reshape(1),
        part(0, 0),
        received,
        weight_now,
        moment_one[0],
        moment_two[0],
        far,
    )
    return (updated[None], first[None], second[None])


def solution(mesh):
    inner = Mesh(mesh.devices.reshape(NY, NH, NZ, NX, NC), ("y", "h", "z", "x", "c"))
    dp, expert = ("y", "h"), ("z", "x", "c")
    placed = (
        P(dp + expert, None),
        P(dp + expert, None),
        P(dp + expert, None),
        P(dp + expert),
        P(),
        P(expert, dp, None),
        P(expert, dp, None),
        P(expert, dp, None),
        P(),
    )
    return jax.shard_map(
        body,
        mesh=inner,
        in_specs=placed,
        out_specs=(P(expert, dp, None),) * 3,
        check_vma=False,
    )
```

```python
import functools
import math

import jax
import jax.numpy as jnp
from jax import lax
from jax.experimental import pallas as pl
from jax.experimental.pallas import tpu as pltpu
from jax.sharding import Mesh, PartitionSpec as P

beta_one = 0.9
beta_two = 0.95
learn_rate = 0.02
epsilon = 1e-08
decay_rate = 0.1
adam_step = 10.0

NY, NH, NZ, NX, NC = 4, 2, 16, 2, 2
CAP = 18
TOK, D, FF = 128, 2048, 768
SHARD = D // (NY * NH)
META = 8
WIDE = D + 128
RELS = ((0, 0), (0, 1), (1, 0), (1, 1))
GROUPS = (((0, 1, -1, 2, -2, 3, -3),), ((4, -4, 5, -5),), ((6, -6, 7, -7, 8),))
TILE = 512
PICK_TILE = 1024
INV_ROOT = 1.0 / math.sqrt(D)
CUTS = (7 * SHARD // 16, 9 * SHARD // 16)
VMEM_LIMIT = 56 * 1024 * 1024


def rows_of(count):
    return -(-count * CAP // 16) * 16


def shift_z(block, distance):
    return lax.ppermute(block, "z", [(i, (i + distance) % NZ) for i in range(NZ)])


def swap_xc(block, dx, dc):
    pairs = [
        (x * NC + c, (x ^ dx) * NC + (c ^ dc)) for x in range(NX) for c in range(NC)
    ]
    return lax.ppermute(block, ("x", "c"), pairs)


def silu_slope(preact):
    sigmoid_val = jax.nn.sigmoid(preact)
    return sigmoid_val * (1.0 + preact * (1.0 - sigmoid_val))


def cast_kernel(one_ref, two_ref, *outs):
    at = 0
    for out in outs:
        rows = out.shape[1]
        out[0] = one_ref[at : at + rows, :].astype(jnp.bfloat16)
        out[1] = two_ref[at : at + rows, :].astype(jnp.bfloat16)
        at += rows


def cast_moments(one, two):
    step = FF // 2
    return pl.pallas_call(
        cast_kernel,
        out_shape=[jax.ShapeDtypeStruct((2, rows, FF), jnp.bfloat16) for rows in CUTS],
        grid=(FF // step,),
        in_specs=[pl.BlockSpec((SHARD, step), lambda i: (0, i))] * 2,
        out_specs=[pl.BlockSpec((2, rows, step), lambda i: (0, 0, i)) for rows in CUTS],
        compiler_params=pltpu.CompilerParams(vmem_limit_bytes=VMEM_LIMIT),
        cost_estimate=pl.CostEstimate(
            flops=2 * SHARD * FF, bytes_accessed=12 * SHARD * FF, transcendentals=0
        ),
        name="cast",
    )(one, two)


def adam_kernel(flag_ref, parts_ref, weight_ref, one_ref, two_ref, far_a, far_b, *outs):
    updated_ref, first_ref, second_ref = outs
    total = parts_ref[0].astype(jnp.float32)
    for i in range(1, parts_ref.shape[0]):
        total = total + parts_ref[i].astype(jnp.float32)
    gradient = total.T
    swapped = flag_ref[0] == 1
    rows = gradient.shape[0]
    rest = rows - far_a.shape[1]
    low = jnp.concatenate([far_a[...], far_b[:, :rest]], axis=1).astype(jnp.float32)
    high = far_b[:, rest:].astype(jnp.float32)
    far = jnp.where(pl.program_id(0) == 0, low, high)
    first_now = jnp.where(swapped, far[0], one_ref[...])
    second_now = jnp.where(swapped, far[1], two_ref[...])
    first = beta_one * first_now + (1.0 - beta_one) * gradient
    second = beta_two * second_now + (1.0 - beta_two) * gradient * gradient
    first_hat = first / (1.0 - beta_one**adam_step)
    second_hat = second / (1.0 - beta_two**adam_step)
    old_weight = weight_ref[...].astype(jnp.float32)
    updated_ref[...] = (
        old_weight
        - learn_rate * (first_hat / (jnp.sqrt(second_hat) + epsilon) + decay_rate * old_weight)
    ).astype(jnp.bfloat16)
    first_ref[...] = first
    second_ref[...] = second


def adam(flag, parts, weight, one, two, far):
    step = SHARD // 2
    plain = pl.BlockSpec((step, FF), lambda i: (i, 0))
    whole = [pl.BlockSpec(f.shape, lambda i: (0, 0, 0)) for f in far]
    return pl.pallas_call(
        adam_kernel,
        out_shape=[
            jax.ShapeDtypeStruct((SHARD, FF), jnp.bfloat16),
            jax.ShapeDtypeStruct((SHARD, FF), jnp.float32),
            jax.ShapeDtypeStruct((SHARD, FF), jnp.float32),
        ],
        grid=(SHARD // step,),
        in_specs=[pl.BlockSpec(memory_space=pltpu.SMEM)]
        + [pl.BlockSpec((parts.shape[0], FF, step), lambda i: (0, 0, i))]
        + [plain, plain, plain]
        + whole,
        out_specs=[plain] * 3,
        compiler_params=pltpu.CompilerParams(vmem_limit_bytes=VMEM_LIMIT),
        cost_estimate=pl.CostEstimate(
            flops=30 * SHARD * FF, bytes_accessed=40 * SHARD * FF, transcendentals=SHARD * FF
        ),
        name="adam",
    )(flag, parts, weight, one, two, *far)


def pick_plan(homes, facts, rows):
    count = len(facts)
    masks, gains = [], []
    for home in homes:
        for routes, factors in facts:
            hot = routes == home
            masks.append(jnp.max(jnp.where(hot, 1.0, 0.0), axis=0, keepdims=True))
            gains.append(jnp.sum(jnp.where(hot, factors, 0.0), axis=0, keepdims=True))
    mask = jnp.concatenate(masks, axis=0)
    earlier = (
        lax.broadcasted_iota(jnp.int32, (TOK, TOK), 0)
        < lax.broadcasted_iota(jnp.int32, (TOK, TOK), 1)
    )
    rank = jnp.dot(
        mask.astype(jnp.bfloat16),
        jnp.where(earlier, 1.0, 0.0).astype(jnp.bfloat16),
        preferred_element_type=jnp.float32,
    )
    slots = lax.broadcasted_iota(jnp.int32, (rows, TOK), 0).astype(jnp.float32)
    selects, totals = [], []
    for i in range(len(homes)):
        lanes, total = [], jnp.zeros((rows, 1), jnp.float32)
        for b in range(count):
            at = i * count + b
            slot = jnp.where(mask[at : at + 1] > 0.0, rank[at : at + 1] + float(b * CAP), -1.0)
            one = jnp.where(slots == slot, 1.0, 0.0)
            total = total + jnp.sum(one * gains[at], axis=1, keepdims=True)
            lanes.append(one.astype(jnp.bfloat16))
        selects.append(jnp.concatenate(lanes, axis=1))
        totals.append(total)
    return jnp.concatenate(selects, axis=0), totals


def select_kernel(cuts, home_ref, *refs):
    n_in = sum(sum(cut) for cut in cuts)
    ins, outs, plans = refs[:n_in], refs[n_in : n_in + 4], refs[n_in + 4 : -1]
    gain_ref = refs[-1]
    step = pl.program_id(0)

    @pl.when(step == 0)
    def _():
        homes = [home_ref[i].astype(jnp.float32) for i in range(4)]
        at = row = 0
        for cut, plan in zip(cuts, plans):
            facts = []
            for n in cut:
                tail = ins[at + n - 1]
                found = tail[tail.shape[0] - META :, 0 : 2 * TOK].astype(jnp.float32)
                facts.append((found[:, :TOK], found[:, TOK:]))
                at += n
            rows = rows_of(len(cut))
            chosen, totals = pick_plan(homes, facts, rows)
            plan[...] = chosen
            for i in range(4):
                gain_ref[i, row : row + rows, :] = jnp.broadcast_to(
                    totals[i], (rows, WIDE - D)
                ).astype(jnp.bfloat16)
            row += rows

    @pl.when(step < D // PICK_TILE)
    def _():
        at = row = 0
        for cut, plan in zip(cuts, plans):
            parts = []
            for n in cut:
                parts += [r[0 : TOK // n, :] for r in ins[at : at + n]]
                at += n
            rows = rows_of(len(cut))
            picked = jnp.dot(
                plan[...], jnp.concatenate(parts, axis=0), preferred_element_type=jnp.float32
            ).astype(jnp.bfloat16)
            for i in range(4):
                outs[i][row : row + rows, :] = picked[i * rows : (i + 1) * rows]
            row += rows

    @pl.when(step == D // PICK_TILE)
    def _():
        for i in range(4):
            outs[i][:, 0 : WIDE - D] = gain_ref[i]


def select(products, homes):
    cuts = tuple(tuple(len(b) for b in blocks) for blocks in products)
    sizes = [rows_of(len(blocks)) for blocks in products]
    rows = sum(sizes)
    flat = [a for blocks in products for b in blocks for a in b]
    last = D // PICK_TILE - 1
    return pl.pallas_call(
        functools.partial(select_kernel, cuts),
        out_shape=[jax.ShapeDtypeStruct((rows, WIDE), jnp.bfloat16)] * 4,
        grid=(D // PICK_TILE + 1,),
        in_specs=[pl.BlockSpec(memory_space=pltpu.SMEM)]
        + [
            pl.BlockSpec((a.shape[0], PICK_TILE), lambda j: (0, jnp.minimum(j, last))) for a in flat
        ],
        out_specs=[pl.BlockSpec((rows, PICK_TILE), lambda j: (0, j))] * 4,
        scratch_shapes=[
            pltpu.VMEM((4 * size, len(blocks) * TOK), jnp.bfloat16)
            for size, blocks in zip(sizes, products)
        ]
        + [pltpu.VMEM((4, rows, WIDE - D), jnp.bfloat16)],
        compiler_params=pltpu.CompilerParams(
            vmem_limit_bytes=VMEM_LIMIT, dimension_semantics=("arbitrary",)
        ),
        cost_estimate=pl.CostEstimate(
            flops=sum(8 * s * len(b) * TOK * D for s, b in zip(sizes, products)),
            bytes_accessed=2 * D * (sum(a.shape[0] for a in flat) + 4 * rows),
            transcendentals=0,
        ),
        name="select",
    )(homes, *flat)


def slopes_kernel(*refs):
    pieces, gains, weight_ref, readout_ref, out_ref, total = refs[:4], refs[4:8], *refs[8:]
    step, steps = pl.program_id(0), pl.num_programs(0)
    rows = jnp.concatenate([p[...] for p in pieces], axis=0)
    product = jnp.dot(rows, weight_ref[...], preferred_element_type=jnp.float32)

    @pl.when(step == 0)
    def _():
        total[...] = product

    @pl.when(step == steps - 1)
    def _():
        factor = jnp.concatenate([g[:, 0:1] for g in gains], axis=0).astype(jnp.float32)
        slope = factor * readout_ref[...] * silu_slope((total[...] + product) * INV_ROOT)
        out_ref[...] = slope.T.astype(jnp.bfloat16)


def slopes_of(pieces, weight_full, readout_row):
    rows = 4 * pieces[0].shape[0]
    step = D // 2
    return pl.pallas_call(
        slopes_kernel,
        out_shape=jax.ShapeDtypeStruct((FF, rows), jnp.bfloat16),
        grid=(2,),
        in_specs=[pl.BlockSpec((p.shape[0], step), lambda j: (0, j)) for p in pieces]
        + [pl.BlockSpec((p.shape[0], WIDE - D), lambda j: (0, D // (WIDE - D))) for p in pieces]
        + [pl.BlockSpec((step, FF), lambda j: (j, 0)), pl.BlockSpec((1, FF), lambda j: (0, 0))],
        out_specs=pl.BlockSpec((FF, rows), lambda j: (0, 0)),
        scratch_shapes=[pltpu.VMEM((rows, FF), jnp.float32)],
        compiler_params=pltpu.CompilerParams(
            vmem_limit_bytes=VMEM_LIMIT, dimension_semantics=("arbitrary",)
        ),
        cost_estimate=pl.CostEstimate(
            flops=2 * rows * D * FF,
            bytes_accessed=2 * (D * FF + rows * (D + FF)),
            transcendentals=rows * FF,
        ),
        name="slopes",
    )(*pieces, *pieces, weight_full, readout_row)


def partial_kernel(n_pieces, *refs):
    pieces, slopes, out_ref = refs[:n_pieces], refs[n_pieces:-1], refs[-1]
    down = jnp.concatenate([s[...] for s in slopes], axis=1)
    rows = jnp.concatenate([p[...] for p in pieces], axis=0)
    total = jnp.dot(down, rows, preferred_element_type=jnp.float32)
    for i in range(TILE // SHARD):
        out_ref[i] = total[:, i * SHARD : (i + 1) * SHARD]


def partial_gradient(pieces, slopes):
    rows = sum(p.shape[0] for p in pieces)
    return pl.pallas_call(
        functools.partial(partial_kernel, len(pieces)),
        out_shape=jax.ShapeDtypeStruct((D // SHARD, FF, SHARD), jnp.float32),
        grid=(D // TILE,),
        in_specs=[pl.BlockSpec((p.shape[0], TILE), lambda j: (0, j)) for p in pieces]
        + [pl.BlockSpec(s.shape, lambda j: (0, 0)) for s in slopes],
        out_specs=pl.BlockSpec((TILE // SHARD, FF, SHARD), lambda j: (j, 0, 0)),
        compiler_params=pltpu.CompilerParams(vmem_limit_bytes=VMEM_LIMIT),
        cost_estimate=pl.CostEstimate(
            flops=2 * rows * D * FF,
            bytes_accessed=2 * rows * (D + FF) + 4 * D * FF,
            transcendentals=0,
        ),
        name="partial",
    )(*pieces, *slopes)


def gradient_kernel(n_pieces, early_ref, slopes_ref, *refs):
    pieces, out_ref = refs[:n_pieces], refs[n_pieces]
    rows = jnp.concatenate([p[...] for p in pieces], axis=0)
    late = jnp.dot(slopes_ref[...], rows, preferred_element_type=jnp.float32)
    for i in range(TILE // SHARD):
        part = late[:, i * SHARD : (i + 1) * SHARD] + early_ref[i]
        out_ref[i] = (part * INV_ROOT).astype(jnp.bfloat16)


def gradient_parts(early, pieces, slopes):
    rows = slopes.shape[1]
    shards = pl.BlockSpec((TILE // SHARD, FF, SHARD), lambda j: (j, 0, 0))
    return pl.pallas_call(
        functools.partial(gradient_kernel, len(pieces)),
        out_shape=jax.ShapeDtypeStruct((D // SHARD, FF, SHARD), jnp.bfloat16),
        grid=(D // TILE,),
        in_specs=[shards, pl.BlockSpec(slopes.shape, lambda j: (0, 0))]
        + [pl.BlockSpec((p.shape[0], TILE), lambda j: (0, j)) for p in pieces],
        out_specs=shards,
        compiler_params=pltpu.CompilerParams(vmem_limit_bytes=VMEM_LIMIT),
        cost_estimate=pl.CostEstimate(
            flops=2 * rows * D * FF,
            bytes_accessed=2 * rows * (D + FF) + 6 * D * FF,
            transcendentals=0,
        ),
        name="gradient",
    )(early, slopes, *pieces)


def body(
    activations, routes, gate_probs, advantage, readout, weights, moment_one, moment_two, swap_flags
):
    experts = NZ * NX * NC
    half = experts // 2
    z, x, c = lax.axis_index("z"), lax.axis_index("x"), lax.axis_index("c")
    y, h = lax.axis_index("y"), lax.axis_index("h")

    def home(dx, dc):
        index = (z * NX + (x ^ dx)) * NC + (c ^ dc)
        flag = lax.dynamic_index_in_dim(swap_flags, index, 0, keepdims=False)
        return (index + flag * half) % experts, flag

    resident, my_flag = home(0, 0)
    homes = jnp.stack([home(dx, dc)[0] for dx, dc in RELS])

    factor = (advantage[:, None] * gate_probs).astype(jnp.bfloat16)
    facts = jnp.concatenate([routes.astype(jnp.bfloat16).T, factor.T], axis=1)
    facts = jnp.pad(facts, ((0, 0), (0, D - 2 * TOK)))
    block = jnp.concatenate([activations, facts], axis=0)
    weight_own = weights[0]
    weight_far = shift_z(weight_own, NZ // 2)
    moments = cast_moments(moment_one[0], moment_two[0])
    readout_row = lax.dynamic_index_in_dim(readout, resident, 0).astype(jnp.float32)

    blocks = {0: (block,)}
    fwd = bwd = block
    picked, pieces, slopes, far = [], [], [], []

    def pick(group):
        picked.append(select([[blocks[o] for o in part] for part in group], homes))

    def exchange():
        pieces.append(
            [p if rel == (0, 0) else swap_xc(p, *rel) for p, rel in zip(picked[-1], RELS)]
        )

    for k in range(1, NZ // 2):
        fwd = shift_z(fwd, 1)
        bwd = shift_z(bwd, -1)
        beside = {
            1: (moments, weight_far, readout_row),
            4: picked[-1:],
            6: pieces[0][2:3] if pieces else (),
            7: pieces[0][1:2] + pieces[0][3:] + pieces[1][2:3] if len(pieces) > 1 else (),
        }.get(k, ())
        if k == 6:
            beside = (beside, picked[1])
        fwd, bwd, beside = lax.optimization_barrier((fwd, bwd, beside))
        blocks[-k] = (fwd,)
        blocks[k] = (bwd,)
        if k == 1:
            moments, weight_far, readout_row = beside
            weight_now = jnp.where(my_flag == 1, weight_far, weight_own)
            weight_full = lax.all_gather(weight_now, ("y", "h"), axis=0, tiled=True)
        elif k == 3:
            pick(GROUPS[0])
        elif k == 4:
            picked[-1] = beside[0]
            exchange()
        elif k == 5:
            pick(GROUPS[1])
        elif k == 6:
            (pieces[0][2],), picked[1] = beside
            exchange()
        elif k == 7:
            pieces[0][1], pieces[0][3], pieces[1][2] = beside
    last = (shift_z(fwd[: TOK // 2], 1), shift_z(bwd[TOK // 2 :], -1))
    slopes = [slopes_of(pieces[0], weight_full, readout_row)]
    rest = [pieces[1][1], pieces[1][3]]
    last, moments, slopes, rest = lax.optimization_barrier((last, moments, slopes, rest))
    pieces[1][1], pieces[1][3] = rest
    blocks[8] = last
    far = [shift_z(m, NZ // 2) for m in moments]
    pick(GROUPS[2])
    exchange()
    slopes.append(slopes_of(pieces[1], weight_full, readout_row))
    early = partial_gradient(pieces[0] + pieces[1], slopes)
    late = slopes_of(pieces[2], weight_full, readout_row)
    late, early = lax.optimization_barrier((late, early))

    parts = gradient_parts(early, pieces[2], late)
    parts, far[0] = lax.optimization_barrier((parts, far[0]))
    received = lax.all_to_all(parts, ("y", "h"), split_axis=0, concat_axis=0, tiled=True)
    updated, first, second = adam(
        my_flag.reshape(1),
        received,
        weight_now,
        moment_one[0],
        moment_two[0],
        far,
    )
    return (updated[None], first[None], second[None])


def solution(mesh):
    inner = Mesh(mesh.devices.reshape(NY, NH, NZ, NX, NC), ("y", "h", "z", "x", "c"))
    dp, expert = ("y", "h"), ("z", "x", "c")
    placed = (
        P(dp + expert, None),
        P(dp + expert, None),
        P(dp + expert, None),
        P(dp + expert),
        P(),
        P(expert, dp, None),
        P(expert, dp, None),
        P(expert, dp, None),
        P(),
    )
    return jax.shard_map(
        body,
        mesh=inner,
        in_specs=placed,
        out_specs=(P(expert, dp, None),) * 3,
        check_vma=False,
    )
```

```python
import functools
import math

import jax
import jax.numpy as jnp
from jax import lax
from jax.experimental import pallas as pl
from jax.experimental.pallas import tpu as pltpu
from jax.sharding import Mesh, PartitionSpec as P

beta_one = 0.9
beta_two = 0.95
learn_rate = 0.02
epsilon = 1e-08
decay_rate = 0.1
adam_step = 10.0

NY, NH, NZ, NX, NC = 4, 2, 16, 2, 2
CAP = 18
TOK, D, FF = 128, 2048, 768
SHARD = D // (NY * NH)
META = 8
WIDE = D + 128
RELS = ((0, 0), (0, 1), (1, 0), (1, 1))
GROUPS = (((0, 1, -1, 2, -2, 3, -3),), ((4, -4, 5, -5),), ((6, -6, 7, -7, 8),))
TILE = 512
PICK_TILE = 1024
INV_ROOT = 1.0 / math.sqrt(D)
AHEAD = 3 * SHARD // 16
VMEM_LIMIT = 56 * 1024 * 1024


def rows_of(count):
    return -(-count * CAP // 16) * 16


def shift_z(block, distance):
    return lax.ppermute(block, "z", [(i, (i + distance) % NZ) for i in range(NZ)])


def traded(flag, block):
    return lax.cond(flag == 1, lambda own: shift_z(own, NZ // 2), lambda own: own, block)


def swap_xc(block, dx, dc):
    pairs = [
        (x * NC + c, (x ^ dx) * NC + (c ^ dc)) for x in range(NX) for c in range(NC)
    ]
    return lax.ppermute(block, ("x", "c"), pairs)


def silu_slope(preact):
    sigmoid_val = jax.nn.sigmoid(preact)
    return sigmoid_val * (1.0 + preact * (1.0 - sigmoid_val))


def cast_kernel(one_ref, two_ref, *outs):
    at = 0
    for out in outs:
        rows = out.shape[1]
        out[0] = one_ref[at : at + rows, :].astype(jnp.bfloat16)
        out[1] = two_ref[at : at + rows, :].astype(jnp.bfloat16)
        at += rows


def cast_moments(one, two):
    step = FF // 2
    cuts = (AHEAD, SHARD - AHEAD)
    return pl.pallas_call(
        cast_kernel,
        out_shape=[jax.ShapeDtypeStruct((2, rows, FF), jnp.bfloat16) for rows in cuts],
        grid=(FF // step,),
        in_specs=[pl.BlockSpec((SHARD, step), lambda i: (0, i))] * 2,
        out_specs=[pl.BlockSpec((2, rows, step), lambda i: (0, 0, i)) for rows in cuts],
        compiler_params=pltpu.CompilerParams(vmem_limit_bytes=VMEM_LIMIT),
        cost_estimate=pl.CostEstimate(
            flops=2 * SHARD * FF, bytes_accessed=12 * SHARD * FF, transcendentals=0
        ),
        name="cast",
    )(one, two)


def adam_kernel(flag_ref, parts_ref, weight_ref, one_ref, two_ref, far_a, far_b, *outs):
    updated_ref, first_ref, second_ref = outs
    total = parts_ref[0].astype(jnp.float32)
    for i in range(1, parts_ref.shape[0]):
        total = total + parts_ref[i].astype(jnp.float32)
    gradient = total.T
    swapped = flag_ref[0] == 1
    rest = gradient.shape[0] - far_a.shape[1]
    low = jnp.concatenate([far_a[...], far_b[:, :rest]], axis=1).astype(jnp.float32)
    high = far_b[:, rest:].astype(jnp.float32)
    far = jnp.where(pl.program_id(0) == 0, low, high)
    first_now = jnp.where(swapped, far[0], one_ref[...])
    second_now = jnp.where(swapped, far[1], two_ref[...])
    first = beta_one * first_now + (1.0 - beta_one) * gradient
    second = beta_two * second_now + (1.0 - beta_two) * gradient * gradient
    first_hat = first / (1.0 - beta_one**adam_step)
    second_hat = second / (1.0 - beta_two**adam_step)
    old_weight = weight_ref[...].astype(jnp.float32)
    updated_ref[...] = (
        old_weight
        - learn_rate * (first_hat / (jnp.sqrt(second_hat) + epsilon) + decay_rate * old_weight)
    ).astype(jnp.bfloat16)
    first_ref[...] = first
    second_ref[...] = second


def adam(flag, parts, weight, one, two, far):
    step = SHARD // 2
    plain = pl.BlockSpec((step, FF), lambda i: (i, 0))
    return pl.pallas_call(
        adam_kernel,
        out_shape=[
            jax.ShapeDtypeStruct((SHARD, FF), jnp.bfloat16),
            jax.ShapeDtypeStruct((SHARD, FF), jnp.float32),
            jax.ShapeDtypeStruct((SHARD, FF), jnp.float32),
        ],
        grid=(SHARD // step,),
        in_specs=[pl.BlockSpec(memory_space=pltpu.SMEM)]
        + [pl.BlockSpec((parts.shape[0], FF, step), lambda i: (0, 0, i))]
        + [plain, plain, plain]
        + [pl.BlockSpec(f.shape, lambda i: (0, 0, 0)) for f in far],
        out_specs=[plain] * 3,
        compiler_params=pltpu.CompilerParams(vmem_limit_bytes=VMEM_LIMIT),
        cost_estimate=pl.CostEstimate(
            flops=30 * SHARD * FF, bytes_accessed=40 * SHARD * FF, transcendentals=SHARD * FF
        ),
        name="adam",
    )(flag, parts, weight, one, two, *far)


def pick_plan(homes, facts, rows):
    count = len(facts)
    masks, gains = [], []
    for home in homes:
        for routes, factors in facts:
            hot = routes == home
            masks.append(jnp.max(jnp.where(hot, 1.0, 0.0), axis=0, keepdims=True))
            gains.append(jnp.sum(jnp.where(hot, factors, 0.0), axis=0, keepdims=True))
    mask = jnp.concatenate(masks, axis=0)
    earlier = (
        lax.broadcasted_iota(jnp.int32, (TOK, TOK), 0)
        < lax.broadcasted_iota(jnp.int32, (TOK, TOK), 1)
    )
    rank = jnp.dot(
        mask.astype(jnp.bfloat16),
        jnp.where(earlier, 1.0, 0.0).astype(jnp.bfloat16),
        preferred_element_type=jnp.float32,
    )
    slots = lax.broadcasted_iota(jnp.int32, (rows, TOK), 0).astype(jnp.float32)
    selects, totals = [], []
    for i in range(len(homes)):
        lanes, total = [], jnp.zeros((rows, 1), jnp.float32)
        for b in range(count):
            at = i * count + b
            slot = jnp.where(mask[at : at + 1] > 0.0, rank[at : at + 1] + float(b * CAP), -1.0)
            one = jnp.where(slots == slot, 1.0, 0.0)
            total = total + jnp.sum(one * gains[at], axis=1, keepdims=True)
            lanes.append(one.astype(jnp.bfloat16))
        selects.append(jnp.concatenate(lanes, axis=1))
        totals.append(total)
    return jnp.concatenate(selects, axis=0), totals


def select_kernel(cuts, home_ref, *refs):
    n_in = sum(sum(cut) for cut in cuts)
    ins, outs, plans = refs[:n_in], refs[n_in : n_in + 4], refs[n_in + 4 : -1]
    gain_ref = refs[-1]
    step = pl.program_id(0)

    @pl.when(step == 0)
    def _():
        homes = [home_ref[i].astype(jnp.float32) for i in range(4)]
        at = row = 0
        for cut, plan in zip(cuts, plans):
            facts = []
            for n in cut:
                tail = ins[at + n - 1]
                found = tail[tail.shape[0] - META :, 0 : 2 * TOK].astype(jnp.float32)
                facts.append((found[:, :TOK], found[:, TOK:]))
                at += n
            rows = rows_of(len(cut))
            chosen, totals = pick_plan(homes, facts, rows)
            plan[...] = chosen
            for i in range(4):
                gain_ref[i, row : row + rows, :] = jnp.broadcast_to(
                    totals[i], (rows, WIDE - D)
                ).astype(jnp.bfloat16)
            row += rows

    @pl.when(step < D // PICK_TILE)
    def _():
        at = row = 0
        for cut, plan in zip(cuts, plans):
            parts = []
            for n in cut:
                parts += [r[0 : TOK // n, :] for r in ins[at : at + n]]
                at += n
            rows = rows_of(len(cut))
            picked = jnp.dot(
                plan[...], jnp.concatenate(parts, axis=0), preferred_element_type=jnp.float32
            ).astype(jnp.bfloat16)
            for i in range(4):
                outs[i][row : row + rows, :] = picked[i * rows : (i + 1) * rows]
            row += rows

    @pl.when(step == D // PICK_TILE)
    def _():
        for i in range(4):
            outs[i][:, 0 : WIDE - D] = gain_ref[i]


def select(products, homes):
    cuts = tuple(tuple(len(b) for b in blocks) for blocks in products)
    sizes = [rows_of(len(blocks)) for blocks in products]
    rows = sum(sizes)
    flat = [a for blocks in products for b in blocks for a in b]
    last = D // PICK_TILE - 1
    return pl.pallas_call(
        functools.partial(select_kernel, cuts),
        out_shape=[jax.ShapeDtypeStruct((rows, WIDE), jnp.bfloat16)] * 4,
        grid=(D // PICK_TILE + 1,),
        in_specs=[pl.BlockSpec(memory_space=pltpu.SMEM)]
        + [
            pl.BlockSpec((a.shape[0], PICK_TILE), lambda j: (0, jnp.minimum(j, last))) for a in flat
        ],
        out_specs=[pl.BlockSpec((rows, PICK_TILE), lambda j: (0, j))] * 4,
        scratch_shapes=[
            pltpu.VMEM((4 * size, len(blocks) * TOK), jnp.bfloat16)
            for size, blocks in zip(sizes, products)
        ]
        + [pltpu.VMEM((4, rows, WIDE - D), jnp.bfloat16)],
        compiler_params=pltpu.CompilerParams(
            vmem_limit_bytes=VMEM_LIMIT, dimension_semantics=("arbitrary",)
        ),
        cost_estimate=pl.CostEstimate(
            flops=sum(8 * s * len(b) * TOK * D for s, b in zip(sizes, products)),
            bytes_accessed=2 * D * (sum(a.shape[0] for a in flat) + 4 * rows),
            transcendentals=0,
        ),
        name="select",
    )(homes, *flat)


def slopes_kernel(n_pieces, *refs):
    pieces, gains = refs[:n_pieces], refs[n_pieces : 2 * n_pieces]
    weight_ref, readout_ref, out_ref, total = refs[2 * n_pieces :]
    step, steps = pl.program_id(0), pl.num_programs(0)
    rows = jnp.concatenate([p[...] for p in pieces], axis=0)
    product = jnp.dot(rows, weight_ref[...], preferred_element_type=jnp.float32)

    @pl.when(step == 0)
    def _():
        total[...] = product

    @pl.when(step == steps - 1)
    def _():
        factor = jnp.concatenate([g[:, 0:1] for g in gains], axis=0).astype(jnp.float32)
        slope = factor * readout_ref[...] * silu_slope((total[...] + product) * INV_ROOT)
        out_ref[...] = slope.T.astype(jnp.bfloat16)


def slopes_of(pieces, weight_full, readout_row):
    rows = sum(p.shape[0] for p in pieces)
    step = D // 2
    return pl.pallas_call(
        functools.partial(slopes_kernel, len(pieces)),
        out_shape=jax.ShapeDtypeStruct((FF, rows), jnp.bfloat16),
        grid=(2,),
        in_specs=[pl.BlockSpec((p.shape[0], step), lambda j: (0, j)) for p in pieces]
        + [pl.BlockSpec((p.shape[0], WIDE - D), lambda j: (0, D // (WIDE - D))) for p in pieces]
        + [pl.BlockSpec((step, FF), lambda j: (j, 0)), pl.BlockSpec((1, FF), lambda j: (0, 0))],
        out_specs=pl.BlockSpec((FF, rows), lambda j: (0, 0)),
        scratch_shapes=[pltpu.VMEM((rows, FF), jnp.float32)],
        compiler_params=pltpu.CompilerParams(
            vmem_limit_bytes=VMEM_LIMIT, dimension_semantics=("arbitrary",)
        ),
        cost_estimate=pl.CostEstimate(
            flops=2 * rows * D * FF,
            bytes_accessed=2 * (D * FF + rows * (D + FF)),
            transcendentals=rows * FF,
        ),
        name="slopes",
    )(*pieces, *pieces, weight_full, readout_row)


def gradient_kernel(n_pieces, *refs):
    pieces, slopes, out_ref = refs[:n_pieces], refs[n_pieces:-1], refs[-1]
    down = jnp.concatenate([s[...] for s in slopes], axis=1)
    rows = jnp.concatenate([p[...] for p in pieces], axis=0)
    total = jnp.dot(down, rows, preferred_element_type=jnp.float32)
    total = (total * INV_ROOT).astype(jnp.bfloat16)
    for i in range(TILE // SHARD):
        out_ref[i] = total[:, i * SHARD : (i + 1) * SHARD]


def gradient_parts(pieces, slopes):
    rows = sum(p.shape[0] for p in pieces)
    return pl.pallas_call(
        functools.partial(gradient_kernel, len(pieces)),
        out_shape=jax.ShapeDtypeStruct((D // SHARD, FF, SHARD), jnp.bfloat16),
        grid=(D // TILE,),
        in_specs=[pl.BlockSpec((p.shape[0], TILE), lambda j: (0, j)) for p in pieces]
        + [pl.BlockSpec(s.shape, lambda j: (0, 0)) for s in slopes],
        out_specs=pl.BlockSpec((TILE // SHARD, FF, SHARD), lambda j: (j, 0, 0)),
        compiler_params=pltpu.CompilerParams(vmem_limit_bytes=VMEM_LIMIT),
        cost_estimate=pl.CostEstimate(
            flops=2 * rows * D * FF,
            bytes_accessed=2 * (rows * (D + FF) + D * FF),
            transcendentals=0,
        ),
        name="gradient",
    )(*pieces, *slopes)


def body(
    activations, routes, gate_probs, advantage, readout, weights, moment_one, moment_two, swap_flags
):
    experts = NZ * NX * NC
    half = experts // 2
    z, x, c = lax.axis_index("z"), lax.axis_index("x"), lax.axis_index("c")
    y, h = lax.axis_index("y"), lax.axis_index("h")

    def home(dx, dc):
        index = (z * NX + (x ^ dx)) * NC + (c ^ dc)
        flag = lax.dynamic_index_in_dim(swap_flags, index, 0, keepdims=False)
        return (index + flag * half) % experts, flag

    resident, my_flag = home(0, 0)
    homes = jnp.stack([home(dx, dc)[0] for dx, dc in RELS])

    factor = (advantage[:, None] * gate_probs).astype(jnp.bfloat16)
    facts = jnp.concatenate([routes.astype(jnp.bfloat16).T, factor.T], axis=1)
    facts = jnp.pad(facts, ((0, 0), (0, D - 2 * TOK)))
    block = jnp.concatenate([activations, facts], axis=0)
    weight_now = traded(my_flag, weights[0])
    moments = cast_moments(moment_one[0], moment_two[0])
    readout_row = lax.dynamic_index_in_dim(readout, resident, 0).astype(jnp.float32)

    blocks = {0: (block,)}
    fwd = bwd = block
    picked, pieces = [], []

    def pick(group):
        picked.append(select([[blocks[o] for o in part] for part in group], homes))

    def exchange():
        pieces.append(
            [p if rel == (0, 0) else swap_xc(p, *rel) for p, rel in zip(picked[-1], RELS)]
        )

    for k in range(1, NZ // 2):
        fwd = shift_z(fwd, 1)
        bwd = shift_z(bwd, -1)
        if k == 1:
            beside = [weight_now, readout_row, *moments]
        elif k == 3:
            beside = [ahead]
        elif k == 4:
            beside = [picked[0]]
        elif k == 6:
            beside = [pieces[0][1], pieces[0][2], picked[1]]
        elif k == 7:
            beside = [pieces[0][3], pieces[1][2]]
        else:
            beside = []
        fwd, bwd, beside = lax.optimization_barrier((fwd, bwd, beside))
        blocks[-k] = (fwd,)
        blocks[k] = (bwd,)
        if k == 1:
            weight_now, readout_row, *moments = beside
            weight_full = lax.all_gather(weight_now, ("y", "h"), axis=0, tiled=True)
            ahead = shift_z(moments[0], NZ // 2)
        elif k == 3:
            (ahead,) = beside
            pick(GROUPS[0])
        elif k == 4:
            (picked[0],) = beside
            exchange()
        elif k == 5:
            pick(GROUPS[1])
        elif k == 6:
            pieces[0][1], pieces[0][2], picked[1] = beside
            exchange()
        elif k == 7:
            pieces[0][3], pieces[1][2] = beside
    last = (shift_z(fwd[: TOK // 2], 1), shift_z(bwd[TOK // 2 :], -1))
    rest = [pieces[1][1], pieces[1][3]]
    last, rest = lax.optimization_barrier((last, rest))
    pieces[1][1], pieces[1][3] = rest
    blocks[8] = last
    pick(GROUPS[2])
    exchange()
    slopes = slopes_of(pieces[0] + pieces[1], weight_full, readout_row)
    slopes, pieces[2] = lax.optimization_barrier((slopes, pieces[2]))
    slopes = [slopes, slopes_of(pieces[2], weight_full, readout_row)]
    parts = gradient_parts([p for group in pieces for p in group], slopes)
    parts, moment_rest = lax.optimization_barrier((parts, moments[1]))
    behind = traded(my_flag, moment_rest)
    received = lax.all_to_all(parts, ("y", "h"), split_axis=0, concat_axis=0, tiled=True)
    updated, first, second = adam(
        my_flag.reshape(1),
        received,
        weight_now,
        moment_one[0],
        moment_two[0],
        (ahead, behind),
    )
    return (updated[None], first[None], second[None])


def solution(mesh):
    inner = Mesh(mesh.devices.reshape(NY, NH, NZ, NX, NC), ("y", "h", "z", "x", "c"))
    dp, expert = ("y", "h"), ("z", "x", "c")
    placed = (
        P(dp + expert, None),
        P(dp + expert, None),
        P(dp + expert, None),
        P(dp + expert),
        P(),
        P(expert, dp, None),
        P(expert, dp, None),
        P(expert, dp, None),
        P(),
    )
    return jax.shard_map(
        body,
        mesh=inner,
        in_specs=placed,
        out_specs=(P(expert, dp, None),) * 3,
        check_vma=False,
    )
```

```python
import functools
import math

import jax
import jax.numpy as jnp
from jax import lax
from jax.experimental import pallas as pl
from jax.experimental.pallas import tpu as pltpu
from jax.sharding import Mesh, PartitionSpec as P

beta_one = 0.9
beta_two = 0.95
learn_rate = 0.02
epsilon = 1e-08
decay_rate = 0.1
adam_step = 10.0

NY, NH, NZ, NX, NC = 4, 2, 16, 2, 2
CAP = 18
TOK, D, FF = 128, 2048, 768
SHARD = D // (NY * NH)
META = 8
WIDE = D + 128
RELS = ((0, 0), (0, 1), (1, 0), (1, 1))
BATCH = 8
TILE = 512
PICK_TILE = 1024
INV_ROOT = 1.0 / math.sqrt(D)
AHEAD = 5 * SHARD // 16
VMEM_LIMIT = 56 * 1024 * 1024


def rows_of(count):
    return -(-count * CAP // 16) * 16


def shift_z(block, distance):
    return lax.ppermute(block, "z", [(i, (i + distance) % NZ) for i in range(NZ)])


def traded(flag, block):
    return lax.cond(flag == 1, lambda own: shift_z(own, NZ // 2), lambda own: own, block)


def swap_xc(block, dx, dc):
    pairs = [
        (x * NC + c, (x ^ dx) * NC + (c ^ dc)) for x in range(NX) for c in range(NC)
    ]
    return lax.ppermute(block, ("x", "c"), pairs)


def silu_slope(preact):
    sigmoid_val = jax.nn.sigmoid(preact)
    return sigmoid_val * (1.0 + preact * (1.0 - sigmoid_val))


def cast_kernel(one_ref, two_ref, *outs):
    at = 0
    for out in outs:
        rows = out.shape[1]
        out[0] = one_ref[at : at + rows, :].astype(jnp.bfloat16)
        out[1] = two_ref[at : at + rows, :].astype(jnp.bfloat16)
        at += rows


def cast_moments(one, two):
    step = FF // 2
    cuts = (AHEAD, SHARD - AHEAD)
    return pl.pallas_call(
        cast_kernel,
        out_shape=[jax.ShapeDtypeStruct((2, rows, FF), jnp.bfloat16) for rows in cuts],
        grid=(FF // step,),
        in_specs=[pl.BlockSpec((SHARD, step), lambda i: (0, i))] * 2,
        out_specs=[pl.BlockSpec((2, rows, step), lambda i: (0, 0, i)) for rows in cuts],
        compiler_params=pltpu.CompilerParams(vmem_limit_bytes=VMEM_LIMIT),
        cost_estimate=pl.CostEstimate(
            flops=2 * SHARD * FF, bytes_accessed=12 * SHARD * FF, transcendentals=0
        ),
        name="cast",
    )(one, two)


def adam_kernel(flag_ref, parts_ref, weight_ref, one_ref, two_ref, far_a, far_b, *outs):
    updated_ref, first_ref, second_ref = outs
    total = parts_ref[0].astype(jnp.float32)
    for i in range(1, parts_ref.shape[0]):
        total = total + parts_ref[i].astype(jnp.float32)
    gradient = total.T
    swapped = flag_ref[0] == 1
    rest = gradient.shape[0] - far_a.shape[1]
    low = jnp.concatenate([far_a[...], far_b[:, :rest]], axis=1).astype(jnp.float32)
    high = far_b[:, rest:].astype(jnp.float32)
    far = jnp.where(pl.program_id(0) == 0, low, high)
    first_now = jnp.where(swapped, far[0], one_ref[...])
    second_now = jnp.where(swapped, far[1], two_ref[...])
    first = beta_one * first_now + (1.0 - beta_one) * gradient
    second = beta_two * second_now + (1.0 - beta_two) * gradient * gradient
    first_hat = first / (1.0 - beta_one**adam_step)
    second_hat = second / (1.0 - beta_two**adam_step)
    old_weight = weight_ref[...].astype(jnp.float32)
    updated_ref[...] = (
        old_weight
        - learn_rate * (first_hat / (jnp.sqrt(second_hat) + epsilon) + decay_rate * old_weight)
    ).astype(jnp.bfloat16)
    first_ref[...] = first
    second_ref[...] = second


def adam(flag, parts, weight, one, two, far):
    step = SHARD // 2
    plain = pl.BlockSpec((step, FF), lambda i: (i, 0))
    return pl.pallas_call(
        adam_kernel,
        out_shape=[
            jax.ShapeDtypeStruct((SHARD, FF), jnp.bfloat16),
            jax.ShapeDtypeStruct((SHARD, FF), jnp.float32),
            jax.ShapeDtypeStruct((SHARD, FF), jnp.float32),
        ],
        grid=(SHARD // step,),
        in_specs=[pl.BlockSpec(memory_space=pltpu.SMEM)]
        + [pl.BlockSpec((parts.shape[0], FF, step), lambda i: (0, 0, i))]
        + [plain, plain, plain]
        + [pl.BlockSpec(f.shape, lambda i: (0, 0, 0)) for f in far],
        out_specs=[plain] * 3,
        compiler_params=pltpu.CompilerParams(vmem_limit_bytes=VMEM_LIMIT),
        cost_estimate=pl.CostEstimate(
            flops=30 * SHARD * FF, bytes_accessed=40 * SHARD * FF, transcendentals=SHARD * FF
        ),
        name="adam",
    )(flag, parts, weight, one, two, *far)


def pick_plan(homes, facts, rows):
    count = len(facts)
    masks, gains = [], []
    for home in homes:
        for routes, factors in facts:
            hot = routes == home
            masks.append(jnp.max(jnp.where(hot, 1.0, 0.0), axis=0, keepdims=True))
            gains.append(jnp.sum(jnp.where(hot, factors, 0.0), axis=0, keepdims=True))
    mask = jnp.concatenate(masks, axis=0)
    earlier = (
        lax.broadcasted_iota(jnp.int32, (TOK, TOK), 0)
        < lax.broadcasted_iota(jnp.int32, (TOK, TOK), 1)
    )
    rank = jnp.dot(
        mask.astype(jnp.bfloat16),
        jnp.where(earlier, 1.0, 0.0).astype(jnp.bfloat16),
        preferred_element_type=jnp.float32,
    )
    slots = lax.broadcasted_iota(jnp.int32, (rows, TOK), 0).astype(jnp.float32)
    selects, totals = [], []
    for i in range(len(homes)):
        lanes, total = [], jnp.zeros((rows, 1), jnp.float32)
        for b in range(count):
            at = i * count + b
            slot = jnp.where(mask[at : at + 1] > 0.0, rank[at : at + 1] + float(b * CAP), -1.0)
            one = jnp.where(slots == slot, 1.0, 0.0)
            total = total + jnp.sum(one * gains[at], axis=1, keepdims=True)
            lanes.append(one.astype(jnp.bfloat16))
        selects.append(jnp.concatenate(lanes, axis=1))
        totals.append(total)
    return jnp.concatenate(selects, axis=0), totals


def select_kernel(home_ref, tokens_ref, *refs):
    outs, plan, gain_ref = refs[:4], refs[4], refs[5]
    rows = outs[0].shape[0]
    step = pl.program_id(0)

    @pl.when(step == 0)
    def _():
        homes = [home_ref[i].astype(jnp.float32) for i in range(4)]
        facts = []
        for b in range(BATCH):
            found = tokens_ref[b, TOK:, 0 : 2 * TOK].astype(jnp.float32)
            facts.append((found[:, :TOK], found[:, TOK:]))
        chosen, totals = pick_plan(homes, facts, rows)
        plan[...] = chosen
        for i in range(4):
            gain_ref[i] = jnp.broadcast_to(totals[i], (rows, WIDE - D)).astype(jnp.bfloat16)

    @pl.when(step < D // PICK_TILE)
    def _():
        source = jnp.concatenate([tokens_ref[b, :TOK, :] for b in range(BATCH)], axis=0)
        picked = jnp.dot(plan[...], source, preferred_element_type=jnp.float32)
        picked = picked.astype(jnp.bfloat16)
        for i in range(4):
            outs[i][...] = picked[i * rows : (i + 1) * rows]

    @pl.when(step == D // PICK_TILE)
    def _():
        for i in range(4):
            outs[i][:, 0 : WIDE - D] = gain_ref[i]


def select(tokens, batch, homes):
    rows = rows_of(BATCH)
    last = D // PICK_TILE - 1
    return pl.pallas_call(
        select_kernel,
        out_shape=[jax.ShapeDtypeStruct((rows, WIDE), jnp.bfloat16)] * 4,
        grid=(D // PICK_TILE + 1,),
        in_specs=[
            pl.BlockSpec(memory_space=pltpu.SMEM),
            pl.BlockSpec(
                (BATCH, TOK + META, PICK_TILE), lambda j: (batch, 0, jnp.minimum(j, last))
            ),
        ],
        out_specs=[pl.BlockSpec((rows, PICK_TILE), lambda j: (0, j))] * 4,
        scratch_shapes=[
            pltpu.VMEM((4 * rows, BATCH * TOK), jnp.bfloat16),
            pltpu.VMEM((4, rows, WIDE - D), jnp.bfloat16),
        ],
        compiler_params=pltpu.CompilerParams(
            vmem_limit_bytes=VMEM_LIMIT, dimension_semantics=("arbitrary",)
        ),
        cost_estimate=pl.CostEstimate(
            flops=8 * rows * BATCH * TOK * D,
            bytes_accessed=2 * D * (BATCH * (TOK + META) + 4 * rows),
            transcendentals=0,
        ),
        name="select",
    )(homes, tokens)


def slopes_kernel(n_pieces, *refs):
    pieces, gains = refs[:n_pieces], refs[n_pieces : 2 * n_pieces]
    weight_ref, readout_ref, out_ref, total = refs[2 * n_pieces :]
    step, steps = pl.program_id(0), pl.num_programs(0)
    rows = jnp.concatenate([p[...] for p in pieces], axis=0)
    product = jnp.dot(rows, weight_ref[...], preferred_element_type=jnp.float32)

    @pl.when(step == 0)
    def _():
        total[...] = product

    @pl.when(step == steps - 1)
    def _():
        factor = jnp.concatenate([g[:, 0:1] for g in gains], axis=0).astype(jnp.float32)
        slope = factor * readout_ref[...] * silu_slope((total[...] + product) * INV_ROOT)
        out_ref[...] = slope.T.astype(jnp.bfloat16)


def slopes_of(pieces, weight_full, readout_row):
    rows = sum(p.shape[0] for p in pieces)
    step = D // 2
    return pl.pallas_call(
        functools.partial(slopes_kernel, len(pieces)),
        out_shape=jax.ShapeDtypeStruct((FF, rows), jnp.bfloat16),
        grid=(2,),
        in_specs=[pl.BlockSpec((p.shape[0], step), lambda j: (0, j)) for p in pieces]
        + [pl.BlockSpec((p.shape[0], WIDE - D), lambda j: (0, D // (WIDE - D))) for p in pieces]
        + [pl.BlockSpec((step, FF), lambda j: (j, 0)), pl.BlockSpec((1, FF), lambda j: (0, 0))],
        out_specs=pl.BlockSpec((FF, rows), lambda j: (0, 0)),
        scratch_shapes=[pltpu.VMEM((rows, FF), jnp.float32)],
        compiler_params=pltpu.CompilerParams(
            vmem_limit_bytes=VMEM_LIMIT, dimension_semantics=("arbitrary",)
        ),
        cost_estimate=pl.CostEstimate(
            flops=2 * rows * D * FF,
            bytes_accessed=2 * (D * FF + rows * (D + FF)),
            transcendentals=rows * FF,
        ),
        name="slopes",
    )(*pieces, *pieces, weight_full, readout_row)


def gradient_kernel(n_pieces, *refs):
    pieces, slopes, out_ref = refs[:n_pieces], refs[n_pieces:-1], refs[-1]
    down = jnp.concatenate([s[...] for s in slopes], axis=1)
    rows = jnp.concatenate([p[...] for p in pieces], axis=0)
    total = jnp.dot(down, rows, preferred_element_type=jnp.float32)
    total = (total * INV_ROOT).astype(jnp.bfloat16)
    for i in range(TILE // SHARD):
        out_ref[i] = total[:, i * SHARD : (i + 1) * SHARD]


def gradient_parts(pieces, slopes):
    rows = sum(p.shape[0] for p in pieces)
    return pl.pallas_call(
        functools.partial(gradient_kernel, len(pieces)),
        out_shape=jax.ShapeDtypeStruct((D // SHARD, FF, SHARD), jnp.bfloat16),
        grid=(D // TILE,),
        in_specs=[pl.BlockSpec((p.shape[0], TILE), lambda j: (0, j)) for p in pieces]
        + [pl.BlockSpec(s.shape, lambda j: (0, 0)) for s in slopes],
        out_specs=pl.BlockSpec((TILE // SHARD, FF, SHARD), lambda j: (j, 0, 0)),
        compiler_params=pltpu.CompilerParams(vmem_limit_bytes=VMEM_LIMIT),
        cost_estimate=pl.CostEstimate(
            flops=2 * rows * D * FF,
            bytes_accessed=2 * (rows * (D + FF) + D * FF),
            transcendentals=0,
        ),
        name="gradient",
    )(*pieces, *slopes)


def body(
    activations, routes, gate_probs, advantage, readout, weights, moment_one, moment_two, swap_flags
):
    experts = NZ * NX * NC
    half = experts // 2
    z, x, c = lax.axis_index("z"), lax.axis_index("x"), lax.axis_index("c")
    y, h = lax.axis_index("y"), lax.axis_index("h")

    def home(dx, dc):
        index = (z * NX + (x ^ dx)) * NC + (c ^ dc)
        flag = lax.dynamic_index_in_dim(swap_flags, index, 0, keepdims=False)
        return (index + flag * half) % experts, flag

    resident, my_flag = home(0, 0)
    homes = jnp.stack([home(dx, dc)[0] for dx, dc in RELS])

    factor = (advantage[:, None] * gate_probs).astype(jnp.bfloat16)
    facts = jnp.concatenate([routes.astype(jnp.bfloat16).T, factor.T], axis=1)
    facts = jnp.pad(facts, ((0, 0), (0, D - 2 * TOK)))
    block = jnp.concatenate([activations, facts], axis=0)
    tokens = lax.all_gather(block, "z", axis=0, tiled=False)

    weight_now = traded(my_flag, weights[0])
    weight_full = lax.all_to_all(
        jnp.broadcast_to(weight_now[None], (NY * NH, SHARD, FF)),
        ("y", "h"),
        split_axis=0,
        concat_axis=0,
        tiled=True,
    ).reshape(D, FF)
    readout_row = lax.dynamic_index_in_dim(readout, resident, 0).astype(jnp.float32)
    moments = cast_moments(moment_one[0], moment_two[0])
    tokens, weight_full, readout_row, moments = lax.optimization_barrier(
        (tokens, weight_full, readout_row, moments)
    )

    pieces = []
    for batch in range(NZ // BATCH):
        picked = select(tokens, batch, homes)
        pieces.append(
            [p if rel == (0, 0) else swap_xc(p, *rel) for p, rel in zip(picked, RELS)]
        )
    ahead = shift_z(moments[0], NZ // 2)
    slopes = slopes_of(pieces[0], weight_full, readout_row)
    slopes, pieces[1] = lax.optimization_barrier((slopes, pieces[1]))
    slopes = [slopes, slopes_of(pieces[1], weight_full, readout_row)]
    parts = gradient_parts(pieces[0] + pieces[1], slopes)
    parts, ahead, moment_rest = lax.optimization_barrier((parts, ahead, moments[1]))
    behind = shift_z(moment_rest, NZ // 2)
    received = lax.all_to_all(parts, ("y", "h"), split_axis=0, concat_axis=0, tiled=True)
    updated, first, second = adam(
        my_flag.reshape(1),
        received,
        weight_now,
        moment_one[0],
        moment_two[0],
        (ahead, behind),
    )
    return (updated[None], first[None], second[None])


def solution(mesh):
    inner = Mesh(mesh.devices.reshape(NY, NH, NZ, NX, NC), ("y", "h", "z", "x", "c"))
    dp, expert = ("y", "h"), ("z", "x", "c")
    placed = (
        P(dp + expert, None),
        P(dp + expert, None),
        P(dp + expert, None),
        P(dp + expert),
        P(),
        P(expert, dp, None),
        P(expert, dp, None),
        P(expert, dp, None),
        P(),
    )
    return jax.shard_map(
        body,
        mesh=inner,
        in_specs=placed,
        out_specs=(P(expert, dp, None),) * 3,
        check_vma=False,
    )
```

```python
import functools
import math

import jax
import jax.numpy as jnp
from jax import lax
from jax.experimental import pallas as pl
from jax.experimental.pallas import tpu as pltpu
from jax.sharding import Mesh, PartitionSpec as P

beta_one = 0.9
beta_two = 0.95
learn_rate = 0.02
epsilon = 1e-08
decay_rate = 0.1
adam_step = 10.0

NY, NH, NZ, NX, NC = 4, 2, 16, 2, 2
CAP = 18
TOK, D, FF = 128, 2048, 768
SHARD = D // (NY * NH)
META = 8
WIDE = D + 128
RELS = ((0, 0), (0, 1), (1, 0), (1, 1))
BATCH = 8
TILE = 512
PICK_TILE = 1024
INV_ROOT = 1.0 / math.sqrt(D)
AHEAD = SHARD // 2
VMEM_LIMIT = 56 * 1024 * 1024


def rows_of(count):
    return -(-count * CAP // 16) * 16


def shift_z(block, distance):
    return lax.ppermute(block, "z", [(i, (i + distance) % NZ) for i in range(NZ)])


def traded(flag, block):
    return lax.cond(flag == 1, lambda own: shift_z(own, NZ // 2), lambda own: own, block)


def swap_xc(block, dx, dc):
    pairs = [
        (x * NC + c, (x ^ dx) * NC + (c ^ dc)) for x in range(NX) for c in range(NC)
    ]
    return lax.ppermute(block, ("x", "c"), pairs)


def silu_slope(preact):
    sigmoid_val = jax.nn.sigmoid(preact)
    return sigmoid_val * (1.0 + preact * (1.0 - sigmoid_val))


def cast_kernel(one_ref, two_ref, *outs):
    at = 0
    for out in outs:
        rows = out.shape[1]
        out[0] = one_ref[at : at + rows, :].astype(jnp.bfloat16)
        out[1] = two_ref[at : at + rows, :].astype(jnp.bfloat16)
        at += rows


def cast_moments(one, two):
    step = FF // 2
    cuts = (AHEAD, SHARD - AHEAD)
    return pl.pallas_call(
        cast_kernel,
        out_shape=[jax.ShapeDtypeStruct((2, rows, FF), jnp.bfloat16) for rows in cuts],
        grid=(FF // step,),
        in_specs=[pl.BlockSpec((SHARD, step), lambda i: (0, i))] * 2,
        out_specs=[pl.BlockSpec((2, rows, step), lambda i: (0, 0, i)) for rows in cuts],
        compiler_params=pltpu.CompilerParams(vmem_limit_bytes=VMEM_LIMIT),
        cost_estimate=pl.CostEstimate(
            flops=2 * SHARD * FF, bytes_accessed=12 * SHARD * FF, transcendentals=0
        ),
        name="cast",
    )(one, two)


def adam_kernel(flag_ref, parts_ref, weight_ref, one_ref, two_ref, far_a, far_b, *outs):
    updated_ref, first_ref, second_ref = outs
    total = parts_ref[0].astype(jnp.float32)
    for i in range(1, parts_ref.shape[0]):
        total = total + parts_ref[i].astype(jnp.float32)
    gradient = total.T
    swapped = flag_ref[0] == 1
    far = jnp.where(pl.program_id(0) == 0, far_a[...], far_b[...]).astype(jnp.float32)
    first_now = jnp.where(swapped, far[0], one_ref[...])
    second_now = jnp.where(swapped, far[1], two_ref[...])
    first = beta_one * first_now + (1.0 - beta_one) * gradient
    second = beta_two * second_now + (1.0 - beta_two) * gradient * gradient
    first_hat = first / (1.0 - beta_one**adam_step)
    second_hat = second / (1.0 - beta_two**adam_step)
    old_weight = weight_ref[...].astype(jnp.float32)
    updated_ref[...] = (
        old_weight
        - learn_rate * (first_hat / (jnp.sqrt(second_hat) + epsilon) + decay_rate * old_weight)
    ).astype(jnp.bfloat16)
    first_ref[...] = first
    second_ref[...] = second


def adam(flag, parts, weight, one, two, far):
    step = SHARD // 2
    plain = pl.BlockSpec((step, FF), lambda i: (i, 0))
    return pl.pallas_call(
        adam_kernel,
        out_shape=[
            jax.ShapeDtypeStruct((SHARD, FF), jnp.bfloat16),
            jax.ShapeDtypeStruct((SHARD, FF), jnp.float32),
            jax.ShapeDtypeStruct((SHARD, FF), jnp.float32),
        ],
        grid=(SHARD // step,),
        in_specs=[pl.BlockSpec(memory_space=pltpu.SMEM)]
        + [pl.BlockSpec((parts.shape[0], FF, step), lambda i: (0, 0, i))]
        + [plain, plain, plain]
        + [pl.BlockSpec(f.shape, lambda i: (0, 0, 0)) for f in far],
        out_specs=[plain] * 3,
        compiler_params=pltpu.CompilerParams(vmem_limit_bytes=VMEM_LIMIT),
        cost_estimate=pl.CostEstimate(
            flops=30 * SHARD * FF, bytes_accessed=40 * SHARD * FF, transcendentals=SHARD * FF
        ),
        name="adam",
    )(flag, parts, weight, one, two, *far)


def pick_plan(homes, facts, rows):
    count = len(facts)
    masks, gains = [], []
    for home in homes:
        for routes, factors in facts:
            hot = routes == home
            masks.append(jnp.max(jnp.where(hot, 1.0, 0.0), axis=0, keepdims=True))
            gains.append(jnp.sum(jnp.where(hot, factors, 0.0), axis=0, keepdims=True))
    mask = jnp.concatenate(masks, axis=0)
    earlier = (
        lax.broadcasted_iota(jnp.int32, (TOK, TOK), 0)
        < lax.broadcasted_iota(jnp.int32, (TOK, TOK), 1)
    )
    rank = jnp.dot(
        mask.astype(jnp.bfloat16),
        jnp.where(earlier, 1.0, 0.0).astype(jnp.bfloat16),
        preferred_element_type=jnp.float32,
    )
    slots = lax.broadcasted_iota(jnp.int32, (rows, TOK), 0).astype(jnp.float32)
    selects, totals = [], []
    for i in range(len(homes)):
        lanes, total = [], jnp.zeros((rows, 1), jnp.float32)
        for b in range(count):
            at = i * count + b
            slot = jnp.where(mask[at : at + 1] > 0.0, rank[at : at + 1] + float(b * CAP), -1.0)
            one = jnp.where(slots == slot, 1.0, 0.0)
            total = total + jnp.sum(one * gains[at], axis=1, keepdims=True)
            lanes.append(one.astype(jnp.bfloat16))
        selects.append(jnp.concatenate(lanes, axis=1))
        totals.append(total)
    return jnp.concatenate(selects, axis=0), totals


def select_kernel(home_ref, tokens_ref, *refs):
    outs, plan, gain_ref = refs[:4], refs[4], refs[5]
    rows = outs[0].shape[0]
    step = pl.program_id(0)

    @pl.when(step == 0)
    def _():
        homes = [home_ref[i].astype(jnp.float32) for i in range(4)]
        facts = []
        for b in range(BATCH):
            found = tokens_ref[b, TOK:, 0 : 2 * TOK].astype(jnp.float32)
            facts.append((found[:, :TOK], found[:, TOK:]))
        chosen, totals = pick_plan(homes, facts, rows)
        plan[...] = chosen
        for i in range(4):
            gain_ref[i] = jnp.broadcast_to(totals[i], (rows, WIDE - D)).astype(jnp.bfloat16)

    @pl.when(step < D // PICK_TILE)
    def _():
        source = jnp.concatenate([tokens_ref[b, :TOK, :] for b in range(BATCH)], axis=0)
        picked = jnp.dot(plan[...], source, preferred_element_type=jnp.float32)
        picked = picked.astype(jnp.bfloat16)
        for i in range(4):
            outs[i][...] = picked[i * rows : (i + 1) * rows]

    @pl.when(step == D // PICK_TILE)
    def _():
        for i in range(4):
            outs[i][:, 0 : WIDE - D] = gain_ref[i]


def select(tokens, batch, homes):
    rows = rows_of(BATCH)
    last = D // PICK_TILE - 1
    return pl.pallas_call(
        select_kernel,
        out_shape=[jax.ShapeDtypeStruct((rows, WIDE), jnp.bfloat16)] * 4,
        grid=(D // PICK_TILE + 1,),
        in_specs=[
            pl.BlockSpec(memory_space=pltpu.SMEM),
            pl.BlockSpec(
                (BATCH, TOK + META, PICK_TILE), lambda j: (batch, 0, jnp.minimum(j, last))
            ),
        ],
        out_specs=[pl.BlockSpec((rows, PICK_TILE), lambda j: (0, j))] * 4,
        scratch_shapes=[
            pltpu.VMEM((4 * rows, BATCH * TOK), jnp.bfloat16),
            pltpu.VMEM((4, rows, WIDE - D), jnp.bfloat16),
        ],
        compiler_params=pltpu.CompilerParams(
            vmem_limit_bytes=VMEM_LIMIT, dimension_semantics=("arbitrary",)
        ),
        cost_estimate=pl.CostEstimate(
            flops=8 * rows * BATCH * TOK * D,
            bytes_accessed=2 * D * (BATCH * (TOK + META) + 4 * rows),
            transcendentals=0,
        ),
        name="select",
    )(homes, tokens)


def slopes_kernel(n_pieces, *refs):
    pieces, gains = refs[:n_pieces], refs[n_pieces : 2 * n_pieces]
    weight_ref, readout_ref, out_ref, total = refs[2 * n_pieces :]
    step, steps = pl.program_id(0), pl.num_programs(0)
    rows = jnp.concatenate([p[...] for p in pieces], axis=0)
    product = jnp.dot(rows, weight_ref[...], preferred_element_type=jnp.float32)

    @pl.when(step == 0)
    def _():
        total[...] = product

    @pl.when(step == steps - 1)
    def _():
        factor = jnp.concatenate([g[:, 0:1] for g in gains], axis=0).astype(jnp.float32)
        slope = factor * readout_ref[...] * silu_slope((total[...] + product) * INV_ROOT)
        out_ref[...] = slope.T.astype(jnp.bfloat16)


def slopes_of(pieces, weight_full, readout_row):
    rows = sum(p.shape[0] for p in pieces)
    step = D // 2
    return pl.pallas_call(
        functools.partial(slopes_kernel, len(pieces)),
        out_shape=jax.ShapeDtypeStruct((FF, rows), jnp.bfloat16),
        grid=(2,),
        in_specs=[pl.BlockSpec((p.shape[0], step), lambda j: (0, j)) for p in pieces]
        + [pl.BlockSpec((p.shape[0], WIDE - D), lambda j: (0, D // (WIDE - D))) for p in pieces]
        + [pl.BlockSpec((step, FF), lambda j: (j, 0)), pl.BlockSpec((1, FF), lambda j: (0, 0))],
        out_specs=pl.BlockSpec((FF, rows), lambda j: (0, 0)),
        scratch_shapes=[pltpu.VMEM((rows, FF), jnp.float32)],
        compiler_params=pltpu.CompilerParams(
            vmem_limit_bytes=VMEM_LIMIT, dimension_semantics=("arbitrary",)
        ),
        cost_estimate=pl.CostEstimate(
            flops=2 * rows * D * FF,
            bytes_accessed=2 * (D * FF + rows * (D + FF)),
            transcendentals=rows * FF,
        ),
        name="slopes",
    )(*pieces, *pieces, weight_full, readout_row)


def gradient_kernel(n_pieces, *refs):
    pieces, slopes, out_ref = refs[:n_pieces], refs[n_pieces:-1], refs[-1]
    down = jnp.concatenate([s[...] for s in slopes], axis=1)
    rows = jnp.concatenate([p[...] for p in pieces], axis=0)
    total = jnp.dot(down, rows, preferred_element_type=jnp.float32)
    total = (total * INV_ROOT).astype(jnp.bfloat16)
    for i in range(TILE // SHARD):
        out_ref[i] = total[:, i * SHARD : (i + 1) * SHARD]


def gradient_parts(pieces, slopes):
    rows = sum(p.shape[0] for p in pieces)
    return pl.pallas_call(
        functools.partial(gradient_kernel, len(pieces)),
        out_shape=jax.ShapeDtypeStruct((D // SHARD, FF, SHARD), jnp.bfloat16),
        grid=(D // TILE,),
        in_specs=[pl.BlockSpec((p.shape[0], TILE), lambda j: (0, j)) for p in pieces]
        + [pl.BlockSpec(s.shape, lambda j: (0, 0)) for s in slopes],
        out_specs=pl.BlockSpec((TILE // SHARD, FF, SHARD), lambda j: (j, 0, 0)),
        compiler_params=pltpu.CompilerParams(vmem_limit_bytes=VMEM_LIMIT),
        cost_estimate=pl.CostEstimate(
            flops=2 * rows * D * FF,
            bytes_accessed=2 * (rows * (D + FF) + D * FF),
            transcendentals=0,
        ),
        name="gradient",
    )(*pieces, *slopes)


def body(
    activations, routes, gate_probs, advantage, readout, weights, moment_one, moment_two, swap_flags
):
    experts = NZ * NX * NC
    half = experts // 2
    z, x, c = lax.axis_index("z"), lax.axis_index("x"), lax.axis_index("c")
    y, h = lax.axis_index("y"), lax.axis_index("h")

    def home(dx, dc):
        index = (z * NX + (x ^ dx)) * NC + (c ^ dc)
        flag = lax.dynamic_index_in_dim(swap_flags, index, 0, keepdims=False)
        return (index + flag * half) % experts, flag

    resident, my_flag = home(0, 0)
    homes = jnp.stack([home(dx, dc)[0] for dx, dc in RELS])

    factor = (advantage[:, None] * gate_probs).astype(jnp.bfloat16)
    facts = jnp.concatenate([routes.astype(jnp.bfloat16).T, factor.T], axis=1)
    facts = jnp.pad(facts, ((0, 0), (0, D - 2 * TOK)))
    block = jnp.concatenate([activations, facts], axis=0)
    tokens = lax.all_gather(block, "z", axis=0, tiled=False)

    weight_now = traded(my_flag, weights[0])
    weight_full = lax.all_to_all(
        jnp.broadcast_to(weight_now[None], (NY * NH, SHARD, FF)),
        ("y", "h"),
        split_axis=0,
        concat_axis=0,
        tiled=True,
    ).reshape(D, FF)
    readout_row = lax.dynamic_index_in_dim(readout, resident, 0).astype(jnp.float32)
    moments = cast_moments(moment_one[0], moment_two[0])
    tokens, weight_full, readout_row, moments = lax.optimization_barrier(
        (tokens, weight_full, readout_row, moments)
    )

    pieces = []
    for batch in range(NZ // BATCH):
        picked = select(tokens, batch, homes)
        pieces.append(
            [p if rel == (0, 0) else swap_xc(p, *rel) for p, rel in zip(picked, RELS)]
        )
    ahead = shift_z(moments[0], NZ // 2)
    slopes = slopes_of(pieces[0], weight_full, readout_row)
    slopes, pieces[1] = lax.optimization_barrier((slopes, pieces[1]))
    slopes = [slopes, slopes_of(pieces[1], weight_full, readout_row)]
    parts = gradient_parts(pieces[0] + pieces[1], slopes)
    parts, ahead, moment_rest = lax.optimization_barrier((parts, ahead, moments[1]))
    behind = shift_z(moment_rest, NZ // 2)
    received = lax.all_to_all(parts, ("y", "h"), split_axis=0, concat_axis=0, tiled=True)
    updated, first, second = adam(
        my_flag.reshape(1),
        received,
        weight_now,
        moment_one[0],
        moment_two[0],
        (ahead, behind),
    )
    return (updated[None], first[None], second[None])


def solution(mesh):
    inner = Mesh(mesh.devices.reshape(NY, NH, NZ, NX, NC), ("y", "h", "z", "x", "c"))
    dp, expert = ("y", "h"), ("z", "x", "c")
    placed = (
        P(dp + expert, None),
        P(dp + expert, None),
        P(dp + expert, None),
        P(dp + expert),
        P(),
        P(expert, dp, None),
        P(expert, dp, None),
        P(expert, dp, None),
        P(),
    )
    return jax.shard_map(
        body,
        mesh=inner,
        in_specs=placed,
        out_specs=(P(expert, dp, None),) * 3,
        check_vma=False,
    )
```

```python
import functools
import math

import jax
import jax.numpy as jnp
from jax import lax
from jax.experimental import pallas as pl
from jax.experimental.pallas import tpu as pltpu
from jax.sharding import Mesh, PartitionSpec as P

beta_one = 0.9
beta_two = 0.95
learn_rate = 0.02
epsilon = 1e-08
decay_rate = 0.1
adam_step = 10.0

NY, NH, NZ, NX, NC = 4, 2, 16, 2, 2
CAP = 18
TOK, D, FF = 128, 2048, 768
SHARD = D // (NY * NH)
META = 8
WIDE = D + 128
RELS = ((0, 0), (0, 1), (1, 0), (1, 1))
BATCH = 8
TILE = 512
PICK_TILE = 1024
INV_ROOT = 1.0 / math.sqrt(D)
AHEAD = 9 * SHARD // 16
VMEM_LIMIT = 56 * 1024 * 1024


def rows_of(count):
    return -(-count * CAP // 16) * 16


def shift_z(block, distance):
    return lax.ppermute(block, "z", [(i, (i + distance) % NZ) for i in range(NZ)])


def traded(flag, block):
    return lax.cond(flag == 1, lambda own: shift_z(own, NZ // 2), lambda own: own, block)


def swap_xc(block, dx, dc):
    pairs = [
        (x * NC + c, (x ^ dx) * NC + (c ^ dc)) for x in range(NX) for c in range(NC)
    ]
    return lax.ppermute(block, ("x", "c"), pairs)


def silu_slope(preact):
    sigmoid_val = jax.nn.sigmoid(preact)
    return sigmoid_val * (1.0 + preact * (1.0 - sigmoid_val))


def cast_kernel(one_ref, two_ref, *outs):
    at = 0
    for out in outs:
        rows = out.shape[1]
        out[0] = one_ref[at : at + rows, :].astype(jnp.bfloat16)
        out[1] = two_ref[at : at + rows, :].astype(jnp.bfloat16)
        at += rows


def cast_moments(one, two):
    step = FF // 2
    cuts = (AHEAD, SHARD - AHEAD)
    return pl.pallas_call(
        cast_kernel,
        out_shape=[jax.ShapeDtypeStruct((2, rows, FF), jnp.bfloat16) for rows in cuts],
        grid=(FF // step,),
        in_specs=[pl.BlockSpec((SHARD, step), lambda i: (0, i))] * 2,
        out_specs=[pl.BlockSpec((2, rows, step), lambda i: (0, 0, i)) for rows in cuts],
        compiler_params=pltpu.CompilerParams(vmem_limit_bytes=VMEM_LIMIT),
        cost_estimate=pl.CostEstimate(
            flops=2 * SHARD * FF, bytes_accessed=12 * SHARD * FF, transcendentals=0
        ),
        name="cast",
    )(one, two)


def adam_kernel(flag_ref, parts_ref, weight_ref, one_ref, two_ref, far_a, far_b, *outs):
    updated_ref, first_ref, second_ref = outs
    total = parts_ref[0].astype(jnp.float32)
    for i in range(1, parts_ref.shape[0]):
        total = total + parts_ref[i].astype(jnp.float32)
    gradient = total.T
    swapped = flag_ref[0] == 1
    far = jnp.concatenate([far_a[...], far_b[...]], axis=1)
    rows = gradient.shape[0]
    far = jnp.where(pl.program_id(0) == 0, far[:, :rows], far[:, rows:]).astype(jnp.float32)
    first_now = jnp.where(swapped, far[0], one_ref[...])
    second_now = jnp.where(swapped, far[1], two_ref[...])
    first = beta_one * first_now + (1.0 - beta_one) * gradient
    second = beta_two * second_now + (1.0 - beta_two) * gradient * gradient
    first_hat = first / (1.0 - beta_one**adam_step)
    second_hat = second / (1.0 - beta_two**adam_step)
    old_weight = weight_ref[...].astype(jnp.float32)
    updated_ref[...] = (
        old_weight
        - learn_rate * (first_hat / (jnp.sqrt(second_hat) + epsilon) + decay_rate * old_weight)
    ).astype(jnp.bfloat16)
    first_ref[...] = first
    second_ref[...] = second


def adam(flag, parts, weight, one, two, far):
    step = SHARD // 2
    plain = pl.BlockSpec((step, FF), lambda i: (i, 0))
    return pl.pallas_call(
        adam_kernel,
        out_shape=[
            jax.ShapeDtypeStruct((SHARD, FF), jnp.bfloat16),
            jax.ShapeDtypeStruct((SHARD, FF), jnp.float32),
            jax.ShapeDtypeStruct((SHARD, FF), jnp.float32),
        ],
        grid=(SHARD // step,),
        in_specs=[pl.BlockSpec(memory_space=pltpu.SMEM)]
        + [pl.BlockSpec((parts.shape[0], FF, step), lambda i: (0, 0, i))]
        + [plain, plain, plain]
        + [pl.BlockSpec(f.shape, lambda i: (0, 0, 0)) for f in far],
        out_specs=[plain] * 3,
        compiler_params=pltpu.CompilerParams(vmem_limit_bytes=VMEM_LIMIT),
        cost_estimate=pl.CostEstimate(
            flops=30 * SHARD * FF, bytes_accessed=40 * SHARD * FF, transcendentals=SHARD * FF
        ),
        name="adam",
    )(flag, parts, weight, one, two, *far)


def pick_plan(homes, facts, rows):
    count = len(facts)
    masks, gains = [], []
    for home in homes:
        for routes, factors in facts:
            hot = routes == home
            masks.append(jnp.max(jnp.where(hot, 1.0, 0.0), axis=0, keepdims=True))
            gains.append(jnp.sum(jnp.where(hot, factors, 0.0), axis=0, keepdims=True))
    mask = jnp.concatenate(masks, axis=0)
    earlier = (
        lax.broadcasted_iota(jnp.int32, (TOK, TOK), 0)
        < lax.broadcasted_iota(jnp.int32, (TOK, TOK), 1)
    )
    rank = jnp.dot(
        mask.astype(jnp.bfloat16),
        jnp.where(earlier, 1.0, 0.0).astype(jnp.bfloat16),
        preferred_element_type=jnp.float32,
    )
    slots = lax.broadcasted_iota(jnp.int32, (rows, TOK), 0).astype(jnp.float32)
    selects, totals = [], []
    for i in range(len(homes)):
        lanes, total = [], jnp.zeros((rows, 1), jnp.float32)
        for b in range(count):
            at = i * count + b
            slot = jnp.where(mask[at : at + 1] > 0.0, rank[at : at + 1] + float(b * CAP), -1.0)
            one = jnp.where(slots == slot, 1.0, 0.0)
            total = total + jnp.sum(one * gains[at], axis=1, keepdims=True)
            lanes.append(one.astype(jnp.bfloat16))
        selects.append(jnp.concatenate(lanes, axis=1))
        totals.append(total)
    return jnp.concatenate(selects, axis=0), totals


def select_kernel(home_ref, tokens_ref, *refs):
    outs, plan, gain_ref = refs[:4], refs[4], refs[5]
    rows = outs[0].shape[0]
    step = pl.program_id(0)

    @pl.when(step == 0)
    def _():
        homes = [home_ref[i].astype(jnp.float32) for i in range(4)]
        facts = []
        for b in range(BATCH):
            found = tokens_ref[b, TOK:, 0 : 2 * TOK].astype(jnp.float32)
            facts.append((found[:, :TOK], found[:, TOK:]))
        chosen, totals = pick_plan(homes, facts, rows)
        plan[...] = chosen
        for i in range(4):
            gain_ref[i] = jnp.broadcast_to(totals[i], (rows, WIDE - D)).astype(jnp.bfloat16)

    @pl.when(step < D // PICK_TILE)
    def _():
        source = jnp.concatenate([tokens_ref[b, :TOK, :] for b in range(BATCH)], axis=0)
        picked = jnp.dot(plan[...], source, preferred_element_type=jnp.float32)
        picked = picked.astype(jnp.bfloat16)
        for i in range(4):
            outs[i][...] = picked[i * rows : (i + 1) * rows]

    @pl.when(step == D // PICK_TILE)
    def _():
        for i in range(4):
            outs[i][:, 0 : WIDE - D] = gain_ref[i]


def select(tokens, batch, homes):
    rows = rows_of(BATCH)
    last = D // PICK_TILE - 1
    return pl.pallas_call(
        select_kernel,
        out_shape=[jax.ShapeDtypeStruct((rows, WIDE), jnp.bfloat16)] * 4,
        grid=(D // PICK_TILE + 1,),
        in_specs=[
            pl.BlockSpec(memory_space=pltpu.SMEM),
            pl.BlockSpec(
                (BATCH, TOK + META, PICK_TILE), lambda j: (batch, 0, jnp.minimum(j, last))
            ),
        ],
        out_specs=[pl.BlockSpec((rows, PICK_TILE), lambda j: (0, j))] * 4,
        scratch_shapes=[
            pltpu.VMEM((4 * rows, BATCH * TOK), jnp.bfloat16),
            pltpu.VMEM((4, rows, WIDE - D), jnp.bfloat16),
        ],
        compiler_params=pltpu.CompilerParams(
            vmem_limit_bytes=VMEM_LIMIT, dimension_semantics=("arbitrary",)
        ),
        cost_estimate=pl.CostEstimate(
            flops=8 * rows * BATCH * TOK * D,
            bytes_accessed=2 * D * (BATCH * (TOK + META) + 4 * rows),
            transcendentals=0,
        ),
        name="select",
    )(homes, tokens)


def slopes_kernel(n_pieces, *refs):
    pieces, gains = refs[:n_pieces], refs[n_pieces : 2 * n_pieces]
    weight_ref, readout_ref, out_ref, total = refs[2 * n_pieces :]
    step, steps = pl.program_id(0), pl.num_programs(0)
    rows = jnp.concatenate([p[...] for p in pieces], axis=0)
    product = jnp.dot(rows, weight_ref[...], preferred_element_type=jnp.float32)

    @pl.when(step == 0)
    def _():
        total[...] = product

    @pl.when(step == steps - 1)
    def _():
        factor = jnp.concatenate([g[:, 0:1] for g in gains], axis=0).astype(jnp.float32)
        slope = factor * readout_ref[...] * silu_slope((total[...] + product) * INV_ROOT)
        out_ref[...] = slope.T.astype(jnp.bfloat16)


def slopes_of(pieces, weight_full, readout_row):
    rows = sum(p.shape[0] for p in pieces)
    step = D // 2
    return pl.pallas_call(
        functools.partial(slopes_kernel, len(pieces)),
        out_shape=jax.ShapeDtypeStruct((FF, rows), jnp.bfloat16),
        grid=(2,),
        in_specs=[pl.BlockSpec((p.shape[0], step), lambda j: (0, j)) for p in pieces]
        + [pl.BlockSpec((p.shape[0], WIDE - D), lambda j: (0, D // (WIDE - D))) for p in pieces]
        + [pl.BlockSpec((step, FF), lambda j: (j, 0)), pl.BlockSpec((1, FF), lambda j: (0, 0))],
        out_specs=pl.BlockSpec((FF, rows), lambda j: (0, 0)),
        scratch_shapes=[pltpu.VMEM((rows, FF), jnp.float32)],
        compiler_params=pltpu.CompilerParams(
            vmem_limit_bytes=VMEM_LIMIT, dimension_semantics=("arbitrary",)
        ),
        cost_estimate=pl.CostEstimate(
            flops=2 * rows * D * FF,
            bytes_accessed=2 * (D * FF + rows * (D + FF)),
            transcendentals=rows * FF,
        ),
        name="slopes",
    )(*pieces, *pieces, weight_full, readout_row)


def gradient_kernel(n_pieces, *refs):
    pieces, slopes, out_ref = refs[:n_pieces], refs[n_pieces:-1], refs[-1]
    down = jnp.concatenate([s[...] for s in slopes], axis=1)
    rows = jnp.concatenate([p[...] for p in pieces], axis=0)
    total = jnp.dot(down, rows, preferred_element_type=jnp.float32)
    total = (total * INV_ROOT).astype(jnp.bfloat16)
    for i in range(TILE // SHARD):
        out_ref[i] = total[:, i * SHARD : (i + 1) * SHARD]


def gradient_parts(pieces, slopes):
    rows = sum(p.shape[0] for p in pieces)
    return pl.pallas_call(
        functools.partial(gradient_kernel, len(pieces)),
        out_shape=jax.ShapeDtypeStruct((D // SHARD, FF, SHARD), jnp.bfloat16),
        grid=(D // TILE,),
        in_specs=[pl.BlockSpec((p.shape[0], TILE), lambda j: (0, j)) for p in pieces]
        + [pl.BlockSpec(s.shape, lambda j: (0, 0)) for s in slopes],
        out_specs=pl.BlockSpec((TILE // SHARD, FF, SHARD), lambda j: (j, 0, 0)),
        compiler_params=pltpu.CompilerParams(vmem_limit_bytes=VMEM_LIMIT),
        cost_estimate=pl.CostEstimate(
            flops=2 * rows * D * FF,
            bytes_accessed=2 * (rows * (D + FF) + D * FF),
            transcendentals=0,
        ),
        name="gradient",
    )(*pieces, *slopes)


def body(
    activations, routes, gate_probs, advantage, readout, weights, moment_one, moment_two, swap_flags
):
    experts = NZ * NX * NC
    half = experts // 2
    z, x, c = lax.axis_index("z"), lax.axis_index("x"), lax.axis_index("c")
    y, h = lax.axis_index("y"), lax.axis_index("h")

    def home(dx, dc):
        index = (z * NX + (x ^ dx)) * NC + (c ^ dc)
        flag = lax.dynamic_index_in_dim(swap_flags, index, 0, keepdims=False)
        return (index + flag * half) % experts, flag

    resident, my_flag = home(0, 0)
    homes = jnp.stack([home(dx, dc)[0] for dx, dc in RELS])

    factor = (advantage[:, None] * gate_probs).astype(jnp.bfloat16)
    facts = jnp.concatenate([routes.astype(jnp.bfloat16).T, factor.T], axis=1)
    facts = jnp.pad(facts, ((0, 0), (0, D - 2 * TOK)))
    block = jnp.concatenate([activations, facts], axis=0)
    tokens = lax.all_gather(block, "z", axis=0, tiled=False)

    weight_now = traded(my_flag, weights[0])
    weight_full = lax.all_to_all(
        jnp.broadcast_to(weight_now[None], (NY * NH, SHARD, FF)),
        ("y", "h"),
        split_axis=0,
        concat_axis=0,
        tiled=True,
    ).reshape(D, FF)
    readout_row = lax.dynamic_index_in_dim(readout, resident, 0).astype(jnp.float32)
    moments = cast_moments(moment_one[0], moment_two[0])
    tokens, weight_full, readout_row, moments = lax.optimization_barrier(
        (tokens, weight_full, readout_row, moments)
    )

    pieces = []
    for batch in range(NZ // BATCH):
        picked = select(tokens, batch, homes)
        pieces.append(
            [p if rel == (0, 0) else swap_xc(p, *rel) for p, rel in zip(picked, RELS)]
        )
    ahead = shift_z(moments[0], NZ // 2)
    slopes = slopes_of(pieces[0], weight_full, readout_row)
    slopes, pieces[1] = lax.optimization_barrier((slopes, pieces[1]))
    slopes = [slopes, slopes_of(pieces[1], weight_full, readout_row)]
    parts = gradient_parts(pieces[0] + pieces[1], slopes)
    parts, ahead, moment_rest = lax.optimization_barrier((parts, ahead, moments[1]))
    behind = shift_z(moment_rest, NZ // 2)
    received = lax.all_to_all(parts, ("y", "h"), split_axis=0, concat_axis=0, tiled=True)
    updated, first, second = adam(
        my_flag.reshape(1),
        received,
        weight_now,
        moment_one[0],
        moment_two[0],
        (ahead, behind),
    )
    return (updated[None], first[None], second[None])


def solution(mesh):
    inner = Mesh(mesh.devices.reshape(NY, NH, NZ, NX, NC), ("y", "h", "z", "x", "c"))
    dp, expert = ("y", "h"), ("z", "x", "c")
    placed = (
        P(dp + expert, None),
        P(dp + expert, None),
        P(dp + expert, None),
        P(dp + expert),
        P(),
        P(expert, dp, None),
        P(expert, dp, None),
        P(expert, dp, None),
        P(),
    )
    return jax.shard_map(
        body,
        mesh=inner,
        in_specs=placed,
        out_specs=(P(expert, dp, None),) * 3,
        check_vma=False,
    )
```
